128 devices in a mesh: gx: 4 (over z_hi, core), gy: 32 (over z_lo, x, y).
Axes of the slice: x: 4, y: 4, z: 4 (z_hi: 2, z_lo: 2; z = z_hi * 2 + z_lo), core: 2. Of those that a mesh axis runs over, the one named last changes fastest.
Arguments:
- node_feats: bfloat16 [163840, 512], P(('gx', 'gy')), may hold values from -6 to 6
- edge_feats: bfloat16 [524288, 512], P(('gx', 'gy')), may hold values from -6 to 6
- senders: int32 [524288], P(('gx', 'gy')), may hold values from 0 to 1791
- receivers: int32 [524288], P(('gx', 'gy')), may hold values from 0 to 1279, as said below
- send_lists: int32 [16384], P(('gx', 'gy')), may hold values from 0 to 1279
- coarse_edges: bfloat16 [20480, 512], P(('gx', 'gy')), may hold values from -6 to 6
- coarse_senders: int32 [20480], P(('gx', 'gy')), may hold values from 0 to 2559
- coarse_receivers: int32 [20480], P(('gx', 'gy')), may hold values from 0 to 2559, as said below
- edge_w1: bfloat16 [1536, 512], replicated, may hold values from -0.15625 to 0.15625
- edge_b1: float32 [512], replicated, may hold values from -4 to 4
- edge_w2: bfloat16 [512, 512], replicated, may hold values from -0.25 to 0.25
- edge_b2: float32 [512], replicated, may hold values from -3 to 3
- edge_gain: float32 [512], replicated, may hold values from 0.5 to 1.5
- edge_shift: float32 [512], replicated, may hold values from -3 to 3
- node_w1: bfloat16 [1024, 512], replicated, may hold values from -0.1875 to 0.1875
- node_b1: float32 [512], replicated, may hold values from -4 to 4
- node_w2: bfloat16 [512, 512], replicated, may hold values from -0.25 to 0.25
- node_b2: float32 [512], replicated, may hold values from -3 to 3
- node_gain: float32 [512], replicated, may hold values from 0.5 to 1.5
- node_shift: float32 [512], replicated, may hold values from -3 to 3
Outputs:
- new_nodes: bfloat16 [163840, 512], P(('gx', 'gy'))
- new_edges: bfloat16 [524288, 512], P(('gx', 'gy'))
- new_coarse: bfloat16 [20480, 512], P(('gx', 'gy'))
The draws below stay inside these ranges and needn't reach their ends.
Inputs may be any that keep to these rules, and one draw needn't show every extreme that they name: Within one device the receivers start at 0, never fall, and rise by at most one from an edge to the next; within each aligned block of 128 of its edges they span at most 128 nodes. `coarse_receivers`: of the 160 coarse edges of one device, at most 3 have receivers c with the same c // 20.
All inputs are finite; a program needn't handle non-finite values.
Results may differ from the reference program's by a relative error of at most 0.003.
The reference program's roundings to bfloat16 on the way count: a program that leaves them out, or rounds other values in their place, can miss the bound.
Values may be sent and summed in bfloat16 or wider, within the bound.
A program may use at most 128 MiB of HBM per device.

```python
import jax
import jax.numpy as jnp
from jax import lax

D = 512
N_DEV = 1280
E_DEV = 4096
HB = 128
CE_DEV = 160
NCD = 20
NODES = 163840
EDGES = 524288
NC = 2560
CEDGES = 20480
CCAP = 3
N_GX = 4
N_GY = 32


def draw_receivers(key, part):
    groups = EDGES // E_DEV
    blocks = E_DEV // 128
    target = max(0, (N_DEV - 129) * 7 // (8 * (blocks - 1)))

    def one_device(dev_key):
        sub_keys = jax.random.split(dev_key, 3)
        full_block = jax.random.randint(sub_keys[0], (), 0, blocks, dtype=jnp.int32)
        counts = jax.random.randint(sub_keys[1], (blocks,), target // 2, target + target // 2 + 1, dtype=jnp.int32)
        counts = jnp.where(jnp.arange(blocks, dtype=jnp.int32) == full_block, 128, counts)
        coin_draws = jax.random.randint(sub_keys[2], (blocks, 128), 0, 128, dtype=jnp.int32)
        step_flags = (coin_draws < counts[:, None]).astype(jnp.int32).reshape(E_DEV)
        placed = jnp.cumsum(step_flags) - step_flags
        return jnp.minimum(placed, N_DEV - 1).astype(jnp.int32)
    return jax.vmap(one_device)(jax.random.split(jax.random.fold_in(key, 5), groups)).reshape(EDGES)


def draw_coarse_receivers(key, part):
    groups = CEDGES // CE_DEV
    slot_total = groups * CCAP
    full_owner = jax.random.randint(jax.random.fold_in(key, 11), (), 0, groups, dtype=jnp.int32)
    slot_ids = jnp.arange(slot_total, dtype=jnp.int32)
    owner_of = slot_ids // CCAP

    def one_device(dev_key):
        sub_keys = jax.random.split(dev_key, 3)
        scores = jax.random.randint(sub_keys[0], (slot_total,), 0, 1 << 16, dtype=jnp.int32) * slot_total + slot_ids
        scores = jnp.where(owner_of == full_owner, -1 - slot_ids, scores)
        slot_order = jnp.argsort(scores, stable=True)
        chosen = slot_order[:CE_DEV].astype(jnp.int32)
        shuffle_scores = jax.random.randint(sub_keys[1], (CE_DEV,), 0, 1 << 16, dtype=jnp.int32) * CE_DEV + jnp.arange(CE_DEV, dtype=jnp.int32)
        chosen = chosen[jnp.argsort(shuffle_scores, stable=True)]
        node_pick = jax.random.randint(sub_keys[2], (CE_DEV,), 0, NCD, dtype=jnp.int32)
        return (chosen // CCAP * NCD + node_pick).astype(jnp.int32)
    return jax.vmap(one_device)(jax.random.split(jax.random.fold_in(key, 7), groups)).reshape(CEDGES)


def touch_ends(array, rng, smallest, largest):
    shape = array.shape
    index_at = [jax.random.randint(jax.random.fold_in(rng, axis), (), 0, shape[axis]) for axis in range(len(shape))]
    array = array.at[tuple(index_at)].set(smallest)
    longest = shape.index(max(shape))
    index_at[longest] = (index_at[longest] + 1) % shape[longest]
    return array.at[tuple(index_at)].set(largest)


def steps_of(stream_key, extent, cuts, least, top_value):
    gain = 1.0
    for axis_at, parts in cuts:
        heights = jax.random.uniform(jax.random.fold_in(jax.random.fold_in(stream_key, 6), axis_at), (parts,), jnp.float32, least / len(cuts), top_value / len(cuts))
        gain = gain * jnp.repeat(jnp.exp(heights), extent[axis_at] // parts).reshape((-1,) + (1,) * (len(extent) - 1 - axis_at))
    return gain


def noise(stream_key, shape, deviation, reach, cuts=(), kind=jnp.bfloat16):
    entries = jax.random.normal(stream_key, shape, jnp.float32) * deviation
    if len(cuts) > 0:
        entries = steps_of(stream_key, shape, cuts, -0.22, 0.18) * entries
    return jnp.clip(entries, min=-reach, max=reach).astype(kind)


def setup_inputs(seed: int = 0) -> dict:
    arg_keys = jax.random.split(jax.random.key(seed), 21)
    return {
        "node_feats": noise(arg_keys[0], (NODES, D), 1.0, 6.0, ((0, 128),)),
        "edge_feats": noise(arg_keys[1], (EDGES, D), 1.0, 6.0, ((0, 128),)),
        "senders": touch_ends(jax.random.randint(arg_keys[2], (EDGES,), 0, N_DEV + 4 * HB), jax.random.fold_in(arg_keys[2], 1), 0, (N_DEV + 4 * HB) - 1).astype(jnp.int32),
        "receivers": draw_receivers(jax.random.fold_in(arg_keys[20], 71), 0),
        "send_lists": touch_ends(jax.random.randint(arg_keys[4], (HB * N_GX * N_GY,), 0, N_DEV), jax.random.fold_in(arg_keys[4], 1), 0, N_DEV - 1).astype(jnp.int32),
        "coarse_edges": noise(arg_keys[5], (CEDGES, D), 1.0, 6.0, ((0, 128),)),
        "coarse_senders": touch_ends(jax.random.randint(arg_keys[6], (CEDGES,), 0, NC), jax.random.fold_in(arg_keys[6], 1), 0, NC - 1).astype(jnp.int32),
        "coarse_receivers": draw_coarse_receivers(jax.random.fold_in(arg_keys[20], 71), 0),
        "edge_w1": noise(arg_keys[8], (3 * D, D), (3 * D) ** -0.5, 0.15625),
        "edge_b1": noise(arg_keys[9], (D,), 1.0, 4.0, (), jnp.float32),
        "edge_w2": noise(arg_keys[10], (D, D), D ** -0.5, 0.25),
        "edge_b2": noise(arg_keys[11], (D,), 0.5, 3.0, (), jnp.float32),
        "edge_gain": jnp.clip(1.0 + 0.1 * jax.random.normal(arg_keys[12], (D,), jnp.float32), 0.5, 1.5),
        "edge_shift": noise(arg_keys[13], (D,), 0.5, 3.0, (), jnp.float32),
        "node_w1": noise(arg_keys[14], (2 * D, D), (2 * D) ** -0.5, 0.1875),
        "node_b1": noise(arg_keys[15], (D,), 1.0, 4.0, (), jnp.float32),
        "node_w2": noise(arg_keys[16], (D, D), D ** -0.5, 0.25),
        "node_b2": noise(arg_keys[17], (D,), 0.5, 3.0, (), jnp.float32),
        "node_gain": jnp.clip(1.0 + 0.1 * jax.random.normal(arg_keys[18], (D,), jnp.float32), 0.5, 1.5),
        "node_shift": noise(arg_keys[19], (D,), 0.5, 3.0, (), jnp.float32),
    }


def layer_norm(values, gain_vec, shift_vec):
    row_mean = lax.optimization_barrier(jnp.mean(values, -1, keepdims=True))
    centred = values - row_mean
    variance = lax.optimization_barrier(jnp.mean(centred * centred, -1, keepdims=True))
    return centred * lax.rsqrt(variance + 1e-05) * gain_vec + shift_vec

def edge_update(inputs, edge_rows, w_first, b_first, w_second, b_second, gain_vec, shift_vec):
    pre_act = jnp.dot(inputs, w_first, preferred_element_type=jnp.float32) + b_first
    hidden = jax.nn.silu(pre_act).astype(jnp.bfloat16)
    output = jnp.dot(hidden, w_second, preferred_element_type=jnp.float32) + b_second
    message = layer_norm(output, gain_vec, shift_vec)
    return ((edge_rows.astype(jnp.float32) + message).astype(jnp.bfloat16), message.astype(jnp.bfloat16))

def pick_rows(node_block, index_list):
    return node_block[index_list]

def reference(node_feats, edge_feats, senders, receivers, send_lists, coarse_edges, coarse_senders, coarse_receivers, edge_w1, edge_b1, edge_w2, edge_b2, edge_gain, edge_shift, node_w1, node_b1, node_w2, node_b2, node_gain, node_shift):
    groups = N_GX * N_GY
    nodes3 = node_feats.reshape(groups, N_DEV, D)
    lists = send_lists.reshape(groups, HB)
    boundary = jax.vmap(pick_rows)(nodes3, lists).reshape(N_GX, N_GY, HB, D)
    pieces = [jnp.roll(boundary, 1, 0), jnp.roll(boundary, -1, 0), jnp.roll(boundary, 1, 1), jnp.roll(boundary, -1, 1)]
    node_table = jnp.concatenate([nodes3] + [piece.reshape(groups, HB, D) for piece in pieces], 1)

    def per_device(packed):
        table_rows, edge_rows, send_ids, recv_ids = packed
        inputs = jnp.concatenate([edge_rows, table_rows[send_ids], table_rows[recv_ids]], 1)
        updated, message = edge_update(inputs, edge_rows, edge_w1, edge_b1, edge_w2, edge_b2, edge_gain, edge_shift)
        summed = jax.ops.segment_sum(message.astype(jnp.float32), recv_ids, num_segments=N_DEV)
        return (updated, summed)
    new_edges, fine_sum = lax.map(per_device, (node_table, edge_feats.reshape(groups, E_DEV, D), senders.reshape(groups, E_DEV), receivers.reshape(groups, E_DEV)))
    coarse_nodes = nodes3[:, :NCD].reshape(NC, D)
    coarse_in = jnp.concatenate([coarse_edges, coarse_nodes[coarse_senders], coarse_nodes[coarse_receivers]], 1)
    new_coarse, coarse_msg = edge_update(coarse_in, coarse_edges, edge_w1, edge_b1, edge_w2, edge_b2, edge_gain, edge_shift)
    coarse_sum = jax.ops.segment_sum(coarse_msg.astype(jnp.float32), coarse_receivers, num_segments=NC).reshape(groups, NCD, D)
    fine_sum = fine_sum.at[:, :NCD].add(coarse_sum)

    def per_node(packed):
        node_rows, summed = packed
        inputs = jnp.concatenate([node_rows, summed.astype(jnp.bfloat16)], 1)
        pre_act = jnp.dot(inputs, node_w1, preferred_element_type=jnp.float32) + node_b1
        hidden = jax.nn.silu(pre_act).astype(jnp.bfloat16)
        output = jnp.dot(hidden, node_w2, preferred_element_type=jnp.float32) + node_b2
        return (node_rows.astype(jnp.float32) + layer_norm(output, node_gain, node_shift)).astype(jnp.bfloat16)
    new_nodes = lax.map(per_node, (nodes3, fine_sum)).reshape(NODES, D)
    return (new_nodes, new_edges.reshape(EDGES, D), new_coarse)
```

```python
import functools

import jax
import jax.numpy as jnp
from jax import lax
from jax.experimental import pallas as pl
from jax.experimental.pallas import tpu as pltpu
from jax.sharding import PartitionSpec as P

BF, F32 = jnp.bfloat16, jnp.float32
BLK = 256
WIN = 264


def norm_rows(x, gain, shift):
    mean = jnp.mean(x, -1, keepdims=True)
    c = x - mean
    var = jnp.mean(c * c, -1, keepdims=True)
    return c * lax.rsqrt(var + 1e-05) * gain + shift


def silu(x):
    t = 0.5 * x
    return t + t * jnp.tanh(t)


def fine_kernel(
    snd, rcv,
    edges, node_ref, halo_ref, rcol_a, w1, b1, w2, b2, gain, shift,
    nw1, nb1, nw2, nb2, ngain, nshift,
    new_edges, new_nodes, head,
    p_snd, p_rcv, g_a, g_b, fsum,
    *, esteps, nodes, do_gather=True, do_seg=True, do_mlp=True,
):
    i = pl.program_id(0)
    D = 512

    def gather(block, g):
        if not do_gather:
            return
        base = block * BLK
        for e in range(BLK):
            s = pl.multiple_of(snd[base + e] * 4, 4)
            r = pl.multiple_of(rcv[base + e] * 4, 4)
            g[pl.ds(4 * e, 4), :] = p_snd[pl.ds(s, 4), :] + p_rcv[pl.ds(r, 4), :]

    def project(rows, w_lo, w_hi, table, at, bias):
        n = rows.shape[0]
        for j in range(4):
            v = jnp.dot(rows, w1[w_lo:w_hi, 128 * j:128 * (j + 1)], preferred_element_type=F32)
            if bias is not None:
                v = v + bias[:, 128 * j:128 * (j + 1)]
            table[pl.ds(at * 4 + j, n, stride=4), :] = v

    @pl.when(i == 0)
    def _():
        fsum[...] = jnp.zeros_like(fsum)
        for c in range(nodes // 256):
            rows = node_ref[c * 256:(c + 1) * 256, :]
            project(rows, 512, 1024, p_snd, c * 256, None)
            project(rows, 1024, 1536, p_rcv, c * 256, b1[...])
        for c in range(2):
            project(halo_ref[c * 256:(c + 1) * 256, :], 512, 1024, p_snd, nodes + c * 256, None)
        gather(0, g_a)

    def compute(k, g, block):
        x = edges[pl.ds(k * BLK, BLK), :]
        acc = jnp.dot(x, w1[0:512, :], preferred_element_type=F32)
        pre = acc + jnp.concatenate([g[pl.ds(j, BLK, stride=4), :] for j in range(4)], 1)
        if do_mlp:
            h = silu(pre).astype(BF)
            y = jnp.dot(h, w2[...], preferred_element_type=F32) + b2[...]
            m = norm_rows(y, gain[...], shift[...])
        else:
            m = pre
        new_edges[pl.ds(k * BLK, BLK), :] = (x.astype(F32) + m).astype(BF)
        if do_seg:
            start = pl.multiple_of((rcv[block * BLK] // 8) * 8, 8)
            ids = rcol_a[0, k:k + 1, :]
            hot = (ids - start == lax.broadcasted_iota(jnp.int32, (WIN, BLK), 0)).astype(F32).astype(BF)
            part = jnp.dot(hot, m.astype(BF), preferred_element_type=F32)
            fsum[pl.ds(start, WIN), :] += part

    @pl.when(i < esteps)
    def _():
        gather(2 * i + 1, g_b)
        compute(0, g_a, 2 * i)
        gather(jnp.minimum(2 * i + 2, 2 * esteps - 1), g_a)
        compute(1, g_b, 2 * i + 1)

    @pl.when(i >= esteps)
    def _():
        c = i - esteps
        rows = node_ref[pl.ds(pl.multiple_of(c * 256, 256), 256), :]
        agg = fsum[pl.ds(pl.multiple_of(c * 256, 256), 256), :]
        pre = (
            jnp.dot(rows, nw1[0:512, :], preferred_element_type=F32)
            + jnp.dot(agg.astype(BF), nw1[512:1024, :], preferred_element_type=F32)
            + nb1[...]
        )
        y = jnp.dot(silu(pre).astype(BF), nw2[...], preferred_element_type=F32) + nb2[...]
        new_nodes[...] = (rows.astype(F32) + norm_rows(y, ngain[...], nshift[...])).astype(BF)

    @pl.when(i == esteps)
    def _():
        head[...] = fsum[0:32, :]


def fine_call(snd, rcv, edges, nodes_a, halo, w1, b1, w2, b2, gain, shift, nw1, nb1, nw2, nb2, ngain, nshift, **kw):
    E, D = edges.shape
    N = nodes_a.shape[0]
    esteps = E // (2 * BLK)
    nsteps = N // 256
    rc = rcv.reshape(esteps, 2, BLK)
    row = lambda v: v.reshape(1, D)
    full = lambda s: pl.BlockSpec(s, lambda i, *_: (0,) * len(s))
    return pl.pallas_call(
        functools.partial(fine_kernel, esteps=esteps, nodes=N, **kw),
        out_shape=(
            jax.ShapeDtypeStruct((E, D), BF),
            jax.ShapeDtypeStruct((N, D), BF),
            jax.ShapeDtypeStruct((32, D), F32),
        ),
        grid_spec=pltpu.PrefetchScalarGridSpec(
            num_scalar_prefetch=2,
            grid=(esteps + nsteps,),
            in_specs=[
                pl.BlockSpec((2 * BLK, D), lambda i, *_: (jnp.minimum(i, esteps - 1), 0)),
                full((N, D)), full(halo.shape),
                pl.BlockSpec((1, 2, BLK), lambda i, *_: (jnp.minimum(i, esteps - 1), 0, 0)),
                full((3 * D, D)), full((1, D)), full((D, D)), full((1, D)), full((1, D)), full((1, D)),
                full((2 * D, D)), full((1, D)), full((D, D)), full((1, D)), full((1, D)), full((1, D)),
            ],
            out_specs=(
                pl.BlockSpec((2 * BLK, D), lambda i, *_: (jnp.minimum(i, esteps - 1), 0)),
                pl.BlockSpec((256, D), lambda i, *_: (jnp.maximum(i - esteps, 0), 0)),
                full((32, D)),
            ),
            scratch_shapes=[
                pltpu.VMEM(((N + halo.shape[0]) * 4, 128), F32),
                pltpu.VMEM((N * 4, 128), F32),
                pltpu.VMEM((BLK * 4, 128), F32),
                pltpu.VMEM((BLK * 4, 128), F32),
                pltpu.VMEM((N + WIN, D), F32),
            ],
        ),
        compiler_params=pltpu.CompilerParams(vmem_limit_bytes=60 * 2**20, dimension_semantics=("arbitrary",)),
        cost_estimate=pl.CostEstimate(flops=10 * 10**9, bytes_accessed=14 * 10**6, transcendentals=3 * 10**6),
        name="fine",
    )(snd, rcv, edges, nodes_a, halo, rc, w1, row(b1), w2, row(b2), row(gain), row(shift),
      nw1, row(nb1), nw2, row(nb2), row(ngain), row(nshift))


MESH = pl.DeviceIdType.MESH
NCD = 20
PIECES = ((0, 32), (32, 32), (64, 16))


def coords(a, b):
    return lax.rem(a, 2), (a // 2) * 2 + b // 16, lax.rem(b // 4, 4), lax.rem(b, 4)


def device_at(core, z, x, y):
    return ((z // 2) * 2 + core, lax.rem(z, 2) * 16 + x * 4 + y)


ORDERS = ((3, 2, 1), (2, 1, 3), (1, 3, 2))


def comm_kernel(
    node_ref, lists,
    halo, buf0, buf1, buf2,
    bound, head32,
    send_sem, recv_sem, csend_sem, crecv_sem, hsend_sem, hrecv_sem,
):
    a, b = lax.axis_index("gx"), lax.axis_index("gy")
    me = coords(a, b)
    core = me[0]
    bufs = (buf0, buf1, buf2)

    def peer(axis, step):
        c = list(me)
        c[axis] = lax.rem(c[axis] + step, 4)
        return device_at(*c)

    sibling = (a + 1 - 2 * core, b)
    halo_to = (
        (lax.rem(a + 1, 4), b), (lax.rem(a + 3, 4), b),
        (a, lax.rem(b + 1, 32)), (a, lax.rem(b + 31, 32)),
    )
    partners = [peer(axis, s) for axis in (1, 2, 3) for s in (1, 2, 3)] + [sibling] + list(halo_to)
    barrier = pltpu.get_barrier_semaphore()
    for p in partners:
        pl.semaphore_signal(barrier, inc=1, device_id=p, device_id_type=MESH)

    own = node_ref[0:32, :].astype(F32)
    for j in range(4):
        head32[pl.ds(j, 32, stride=4), :] = own[:, 128 * j:128 * (j + 1)]

    def slot(p):
        o = ORDERS[p]
        return ((core * 4 + me[o[2]]) * 4 + me[o[1]]) * 4 + me[o[0]]

    for p, (r0, n) in enumerate(PIECES):
        bufs[p][slot(p)] = head32[r0:r0 + n, :].astype(BF)

    hot = (lax.broadcasted_iota(jnp.int32, (node_ref.shape[0], 128), 0) == lists[...]).astype(F32).astype(BF)
    bound[...] = lax.dot_general(
        hot, node_ref[...], (((0,), (0,)), ((), ())), preferred_element_type=F32).astype(BF)

    pl.semaphore_wait(barrier, len(partners))

    def hop(p, stage, step):
        o = ORDERS[p]
        size = 4 ** stage
        first = slot(p) // size * size
        part = bufs[p].at[pl.ds(first, size)]
        k = (p * 3 + stage) * 3 + step - 1
        return pltpu.make_async_remote_copy(
            src_ref=part, dst_ref=part, send_sem=send_sem.at[k], recv_sem=recv_sem.at[k],
            device_id=peer(o[stage], step), device_id_type=MESH)

    def across(p, step):
        o = ORDERS[p]
        first = (core * 4 + lax.rem(me[o[2]] + 4 - step, 4)) * 16
        part = bufs[p].at[pl.ds(first, 16)]
        k = p * 4 + step
        return pltpu.make_async_remote_copy(
            src_ref=part, dst_ref=part, send_sem=csend_sem.at[k], recv_sem=crecv_sem.at[k],
            device_id=sibling, device_id_type=MESH)

    started = []

    def go(copy):
        copy.start()
        started.append(copy)
        return copy

    stage = [[go(hop(p, 0, s)) for s in (2, 1, 3)] for p in range(3)]
    halos = []
    for k, to in enumerate(halo_to):
        halos.append(go(pltpu.make_async_remote_copy(
            src_ref=bound, dst_ref=halo.at[pl.ds(128 * k, 128)], send_sem=hsend_sem.at[k], recv_sem=hrecv_sem.at[k],
            device_id=to, device_id_type=MESH)))
    nxt = []
    for p in range(3):
        for c in stage[p]:
            c.wait_recv()
        nxt.append([go(hop(p, 1, s)) for s in (2, 1, 3)])
    stage, nxt, cross = nxt, [], []
    for p in range(3):
        for c in stage[p]:
            c.wait_recv()
        nxt.append([go(hop(p, 2, s)) for s in (2, 1, 3)])
        cross.append(go(across(p, 0)))
    for i, s in enumerate((2, 1, 3)):
        for p in range(3):
            nxt[p][i].wait_recv()
            cross.append(go(across(p, s)))
    for c in cross:
        c.wait_recv()

    for h in halos:
        h.wait_recv()
    for k in started:
        k.wait_send()


def coarse_kernel(
    csnd, crcv,
    buf0, buf1, buf2, cedges, crow, w1, b1, w2, b2, gain, shift,
    new_coarse, outbound,
    table, rows_s, rows_r, wide,
):
    bufs = (buf0, buf1, buf2)

    @pl.loop(0, 128)
    def _(q):
        c, u, v, w = q // 64, lax.rem(q // 16, 4), lax.rem(q // 4, 4), lax.rem(q, 4)
        for p, (r0, n) in enumerate(PIECES):
            pos = {ORDERS[p][2]: u, ORDERS[p][1]: v, ORDERS[p][0]: w}
            aa, bb = device_at(c, pos[1], pos[2], pos[3])
            at = pl.multiple_of((aa * 32 + bb) * 80 + r0, 8)
            table[pl.ds(at, n), :] = bufs[p][q].astype(F32)

    ce = cedges.shape[0]
    for e in range(ce):
        rows_s[pl.ds(4 * e, 4), :] = table[pl.ds(pl.multiple_of(csnd[e] * 4, 4), 4), :]
        rows_r[pl.ds(4 * e, 4), :] = table[pl.ds(pl.multiple_of(crcv[e] * 4, 4), 4), :]
    x = cedges[...]
    take = lambda ref: jnp.concatenate([ref[pl.ds(j, ce, stride=4), :] for j in range(4)], 1).astype(BF)
    pre = (
        jnp.dot(x, w1[0:512, :], preferred_element_type=F32)
        + jnp.dot(take(rows_s), w1[512:1024, :], preferred_element_type=F32)
        + jnp.dot(take(rows_r), w1[1024:1536, :], preferred_element_type=F32)
        + b1[...]
    )
    y = jnp.dot(silu(pre).astype(BF), w2[...], preferred_element_type=F32) + b2[...]
    m = norm_rows(y, gain[...], shift[...])
    new_coarse[...] = (x.astype(F32) + m).astype(BF)
    mb = m.astype(BF)

    c = crow[...]
    owner = lax.shift_right_logical(c * 52429, 20)
    local = c - owner * NCD
    iota = lambda shape, d: lax.broadcasted_iota(jnp.int32, shape, d)
    own_hot = (iota((128, ce), 0) == owner).astype(F32)
    before = (iota((ce, ce), 0) < iota((ce, ce), 1)).astype(F32).astype(BF)
    counts = jnp.dot(own_hot.astype(BF), before, preferred_element_type=F32)
    rank = jnp.sum(own_hot * counts, axis=0, keepdims=True)
    for s in range(3):
        placed = jnp.where(rank == s, own_hot, 0.0).astype(BF)
        got = jnp.dot(placed, mb, preferred_element_type=F32)
        for j in range(4):
            wide[pl.ds(4 * s + j, 128, stride=16), :] = got[:, 128 * j:128 * (j + 1)]
    tags = (iota((128, ce), 0).astype(F32) == rank * 32.0 + local.astype(F32)).astype(F32).astype(BF)
    wide[pl.ds(12, 128, stride=16), :] = lax.dot_general(
        own_hot.astype(BF), tags, (((1,), (1,)), ((), ())), preferred_element_type=F32)
    for j in range(1, 4):
        wide[pl.ds(12 + j, 128, stride=16), :] = jnp.zeros((128, 128), F32)
    outbound[...] = wide[...].astype(BF)


def comm_call(nodes, lists):
    vm = pl.BlockSpec(memory_space=pltpu.VMEM)
    return pl.pallas_call(
        comm_kernel,
        out_shape=(
            jax.ShapeDtypeStruct((512, 512), BF),
            jax.ShapeDtypeStruct((128, 32, 128), BF),
            jax.ShapeDtypeStruct((128, 32, 128), BF),
            jax.ShapeDtypeStruct((128, 16, 128), BF),
        ),
        in_specs=[vm, vm],
        out_specs=(vm,) * 4,
        scratch_shapes=[
            pltpu.VMEM((128, 512), BF),
            pltpu.VMEM((128, 128), F32),
            pltpu.SemaphoreType.DMA((27,)), pltpu.SemaphoreType.DMA((27,)),
            pltpu.SemaphoreType.DMA((12,)), pltpu.SemaphoreType.DMA((12,)),
            pltpu.SemaphoreType.DMA((4,)), pltpu.SemaphoreType.DMA((4,)),
        ],
        compiler_params=pltpu.CompilerParams(
            collective_id=0, has_side_effects=True, vmem_limit_bytes=60 * 2**20),
        cost_estimate=pl.CostEstimate(flops=10**8, bytes_accessed=8 * 10**6, transcendentals=0),
        name="spread",
    )(nodes, lists.reshape(1, -1))


def coarse_call(bufs, cedges, csnd, crcv, w1, b1, w2, b2, gain, shift):
    D = 512
    row = lambda v: v.reshape(1, -1)
    vm = pl.BlockSpec(memory_space=pltpu.VMEM)
    sm = pl.BlockSpec(memory_space=pltpu.SMEM)
    ce = cedges.shape[0]
    return pl.pallas_call(
        coarse_kernel,
        out_shape=(
            jax.ShapeDtypeStruct((ce, D), BF),
            jax.ShapeDtypeStruct((2048, 128), BF),
        ),
        in_specs=[sm, sm] + [vm] * 11,
        out_specs=(vm, vm),
        scratch_shapes=[
            pltpu.VMEM((128 * 80, 128), F32),
            pltpu.VMEM((ce * 4, 128), F32), pltpu.VMEM((ce * 4, 128), F32),
            pltpu.VMEM((2048, 128), F32),
        ],
        compiler_params=pltpu.CompilerParams(vmem_limit_bytes=60 * 2**20),
        cost_estimate=pl.CostEstimate(flops=10**9, bytes_accessed=8 * 10**6, transcendentals=10**5),
        name="coarse",
    )(csnd, crcv, *bufs, cedges, row(crcv), w1, row(b1), w2, row(b2), row(gain), row(shift))


def tail_kernel(node_ref, head, inbound, w1, b1, w2, b2, gain, shift, _, out, wide):
    wide[...] = inbound[...].astype(F32)
    tags = wide[pl.ds(12, 128, stride=16), :].astype(BF)
    total = head[...]
    for s in range(3):
        got = jnp.concatenate([wide[pl.ds(4 * s + j, 128, stride=16), :] for j in range(4)], 1).astype(BF)
        total = total + lax.dot_general(
            tags[:, 32 * s:32 * s + 32], got, (((0,), (0,)), ((), ())), preferred_element_type=F32)
    rows = node_ref[...]
    pre = (
        jnp.dot(rows, w1[0:512, :], preferred_element_type=F32)
        + jnp.dot(total.astype(BF), w1[512:1024, :], preferred_element_type=F32)
        + b1[...]
    )
    y = jnp.dot(silu(pre).astype(BF), w2[...], preferred_element_type=F32) + b2[...]
    out[...] = (rows.astype(F32) + norm_rows(y, gain[...], shift[...])).astype(BF)


def tail_call(nodes, head, inbound, w1, b1, w2, b2, gain, shift, new_nodes):
    D = 512
    row = lambda v: v.reshape(1, D)
    full = lambda s: pl.BlockSpec(s, lambda i: (0,) * len(s))
    return pl.pallas_call(
        tail_kernel,
        out_shape=jax.ShapeDtypeStruct(new_nodes.shape, BF),
        grid=(1,),
        in_specs=[full((32, D)), full((32, D)), full((2048, 128)), full((2 * D, D)), full((1, D)), full((D, D)),
                  full((1, D)), full((1, D)), full((1, D)), pl.BlockSpec(memory_space=pl.ANY)],
        out_specs=full((32, D)),
        scratch_shapes=[pltpu.VMEM((2048, 128), F32)],
        input_output_aliases={9: 0},
        compiler_params=pltpu.CompilerParams(vmem_limit_bytes=48 * 2**20),
        cost_estimate=pl.CostEstimate(flops=10**8, bytes_accessed=3 * 10**6, transcendentals=10**4),
        name="tail",
    )(nodes, head, inbound, w1, row(b1), w2, row(b2), row(gain), row(shift), new_nodes)


AXES = ("gx", "gy")


def on_device(
    node_feats, edge_feats, senders, receivers, send_lists, coarse_edges, coarse_senders, coarse_receivers,
    edge_w1, edge_b1, edge_w2, edge_b2, edge_gain, edge_shift,
    node_w1, node_b1, node_w2, node_b2, node_gain, node_shift,
):
    halo, *bufs = comm_call(node_feats, send_lists)
    new_coarse, outbound = coarse_call(
        bufs, coarse_edges, coarse_senders, coarse_receivers,
        edge_w1, edge_b1, edge_w2, edge_b2, edge_gain, edge_shift)
    inbound = lax.all_to_all(outbound.reshape(128, 16, 128), AXES, 0, 0, tiled=True).reshape(2048, 128)
    new_edges, new_nodes, head = fine_call(
        senders, receivers, edge_feats, node_feats, halo,
        edge_w1, edge_b1, edge_w2, edge_b2, edge_gain, edge_shift,
        node_w1, node_b1, node_w2, node_b2, node_gain, node_shift)
    new_nodes = tail_call(
        node_feats, head, inbound, node_w1, node_b1, node_w2, node_b2, node_gain, node_shift, new_nodes)
    return new_nodes, new_edges, new_coarse


def solution(mesh):
    rows, flat, rep = P(AXES, None), P(AXES), P()
    return jax.shard_map(
        on_device, mesh=mesh,
        in_specs=(rows, rows, flat, flat, flat, rows, flat, flat) + (rep,) * 12,
        out_specs=(rows, rows, rows), check_vma=False,
    )
```

```python
import functools

import jax
import jax.numpy as jnp
from jax import lax
from jax.experimental import pallas as pl
from jax.experimental.pallas import tpu as pltpu
from jax.sharding import PartitionSpec as P

BF, F32 = jnp.bfloat16, jnp.float32
BLK = 256
WIN = 264


def norm_rows(x, gain, shift):
    mean = jnp.mean(x, -1, keepdims=True)
    c = x - mean
    var = jnp.mean(c * c, -1, keepdims=True)
    return c * lax.rsqrt(var + 1e-05) * gain + shift


def silu(x):
    t = 0.5 * x
    return t + t * jnp.tanh(t)


def fine_kernel(
    snd, rcv,
    edges, node_ref, halo_ref, rcol_a, w1, b1, w2, b2, gain, shift,
    nw1, nb1, nw2, nb2, ngain, nshift,
    new_edges, new_nodes, head,
    p_snd, p_rcv, g_a, g_b, fsum,
    *, esteps, nodes, do_gather=True, do_seg=True, do_mlp=True,
):
    i = pl.program_id(0)
    D = 512

    def gather(block, g):
        if not do_gather:
            return
        base = block * BLK
        for e in range(BLK):
            s = pl.multiple_of(snd[base + e] * 4, 4)
            r = pl.multiple_of(rcv[base + e] * 4, 4)
            g[pl.ds(4 * e, 4), :] = p_snd[pl.ds(s, 4), :] + p_rcv[pl.ds(r, 4), :]

    def project(rows, w_lo, w_hi, table, at, bias):
        n = rows.shape[0]
        for j in range(4):
            v = jnp.dot(rows, w1[w_lo:w_hi, 128 * j:128 * (j + 1)], preferred_element_type=F32)
            if bias is not None:
                v = v + bias[:, 128 * j:128 * (j + 1)]
            table[pl.ds(at * 4 + j, n, stride=4), :] = v

    @pl.when(i == 0)
    def _():
        fsum[...] = jnp.zeros_like(fsum)
        for c in range(nodes // 256):
            rows = node_ref[c * 256:(c + 1) * 256, :]
            project(rows, 512, 1024, p_snd, c * 256, None)
            project(rows, 1024, 1536, p_rcv, c * 256, b1[...])
        for c in range(2):
            project(halo_ref[c * 256:(c + 1) * 256, :], 512, 1024, p_snd, nodes + c * 256, None)
        gather(0, g_a)

    def compute(k, g, block):
        x = edges[pl.ds(k * BLK, BLK), :]
        acc = jnp.dot(x, w1[0:512, :], preferred_element_type=F32)
        pre = acc + jnp.concatenate([g[pl.ds(j, BLK, stride=4), :] for j in range(4)], 1)
        if do_mlp:
            h = silu(pre).astype(BF)
            y = jnp.dot(h, w2[...], preferred_element_type=F32) + b2[...]
            m = norm_rows(y, gain[...], shift[...])
        else:
            m = pre
        new_edges[pl.ds(k * BLK, BLK), :] = (x.astype(F32) + m).astype(BF)
        if do_seg:
            start = pl.multiple_of((rcv[block * BLK] // 8) * 8, 8)
            ids = rcol_a[0, k:k + 1, :]
            hot = (ids - start == lax.broadcasted_iota(jnp.int32, (WIN, BLK), 0)).astype(F32).astype(BF)
            part = jnp.dot(hot, m.astype(BF), preferred_element_type=F32)
            fsum[pl.ds(start, WIN), :] += part

    @pl.when(i < esteps)
    def _():
        gather(2 * i + 1, g_b)
        compute(0, g_a, 2 * i)
        gather(jnp.minimum(2 * i + 2, 2 * esteps - 1), g_a)
        compute(1, g_b, 2 * i + 1)

    @pl.when(i >= esteps)
    def _():
        c = i - esteps
        rows = node_ref[pl.ds(pl.multiple_of(c * 256, 256), 256), :]
        agg = fsum[pl.ds(pl.multiple_of(c * 256, 256), 256), :]
        pre = (
            jnp.dot(rows, nw1[0:512, :], preferred_element_type=F32)
            + jnp.dot(agg.astype(BF), nw1[512:1024, :], preferred_element_type=F32)
            + nb1[...]
        )
        y = jnp.dot(silu(pre).astype(BF), nw2[...], preferred_element_type=F32) + nb2[...]
        new_nodes[...] = (rows.astype(F32) + norm_rows(y, ngain[...], nshift[...])).astype(BF)

    @pl.when(i == esteps)
    def _():
        head[...] = fsum[0:32, :]


def fine_call(snd, rcv, edges, nodes_a, halo, w1, b1, w2, b2, gain, shift, nw1, nb1, nw2, nb2, ngain, nshift, **kw):
    E, D = edges.shape
    N = nodes_a.shape[0]
    esteps = E // (2 * BLK)
    nsteps = N // 256
    rc = rcv.reshape(esteps, 2, BLK)
    row = lambda v: v.reshape(1, D)
    full = lambda s: pl.BlockSpec(s, lambda i, *_: (0,) * len(s))
    return pl.pallas_call(
        functools.partial(fine_kernel, esteps=esteps, nodes=N, **kw),
        out_shape=(
            jax.ShapeDtypeStruct((E, D), BF),
            jax.ShapeDtypeStruct((N, D), BF),
            jax.ShapeDtypeStruct((32, D), F32),
        ),
        grid_spec=pltpu.PrefetchScalarGridSpec(
            num_scalar_prefetch=2,
            grid=(esteps + nsteps,),
            in_specs=[
                pl.BlockSpec((2 * BLK, D), lambda i, *_: (jnp.minimum(i, esteps - 1), 0)),
                full((N, D)), full(halo.shape),
                pl.BlockSpec((1, 2, BLK), lambda i, *_: (jnp.minimum(i, esteps - 1), 0, 0)),
                full((3 * D, D)), full((1, D)), full((D, D)), full((1, D)), full((1, D)), full((1, D)),
                full((2 * D, D)), full((1, D)), full((D, D)), full((1, D)), full((1, D)), full((1, D)),
            ],
            out_specs=(
                pl.BlockSpec((2 * BLK, D), lambda i, *_: (jnp.minimum(i, esteps - 1), 0)),
                pl.BlockSpec((256, D), lambda i, *_: (jnp.maximum(i - esteps, 0), 0)),
                full((32, D)),
            ),
            scratch_shapes=[
                pltpu.VMEM(((N + halo.shape[0]) * 4, 128), F32),
                pltpu.VMEM((N * 4, 128), F32),
                pltpu.VMEM((BLK * 4, 128), F32),
                pltpu.VMEM((BLK * 4, 128), F32),
                pltpu.VMEM((N + WIN, D), F32),
            ],
        ),
        compiler_params=pltpu.CompilerParams(vmem_limit_bytes=60 * 2**20, dimension_semantics=("arbitrary",)),
        cost_estimate=pl.CostEstimate(flops=10 * 10**9, bytes_accessed=14 * 10**6, transcendentals=3 * 10**6),
        name="fine",
    )(snd, rcv, edges, nodes_a, halo, rc, w1, row(b1), w2, row(b2), row(gain), row(shift),
      nw1, row(nb1), nw2, row(nb2), row(ngain), row(nshift))


MESH = pl.DeviceIdType.MESH
NCD = 20
PIECES = ((0, 32), (32, 32), (64, 16))


def coords(a, b):
    return lax.rem(a, 2), (a // 2) * 2 + b // 16, lax.rem(b // 4, 4), lax.rem(b, 4)


def device_at(core, z, x, y):
    return ((z // 2) * 2 + core, lax.rem(z, 2) * 16 + x * 4 + y)


ORDERS = ((3, 2, 1), (2, 1, 3), (1, 3, 2))


def comm_kernel(
    csnd, crcv,
    node_ref, lists, cedges, crow, w1, b1, w2, b2, gain, shift,
    halo, new_coarse, outbound,
    buf0, buf1, buf2, table, rows_s, rows_r, wide, bound, head32,
    send_sem, recv_sem, hsend_sem, hrecv_sem,
):
    a, b = lax.axis_index("gx"), lax.axis_index("gy")
    me = coords(a, b)
    core = me[0]
    bufs = (buf0, buf1, buf2)

    def peer(axis, step):
        c = list(me)
        c[axis] = lax.rem(c[axis] + step, 4)
        return device_at(*c)

    sibling = (a + 1 - 2 * core, b)
    halo_to = (
        (lax.rem(a + 1, 4), b), (lax.rem(a + 3, 4), b),
        (a, lax.rem(b + 1, 32)), (a, lax.rem(b + 31, 32)),
    )
    partners = [peer(axis, s) for axis in (1, 2, 3) for s in (1, 2, 3)] + [sibling] + list(halo_to)
    barrier = pltpu.get_barrier_semaphore()
    for p in partners:
        pl.semaphore_signal(barrier, inc=1, device_id=p, device_id_type=MESH)

    own = node_ref[0:32, :].astype(F32)
    for j in range(4):
        head32[pl.ds(j, 32, stride=4), :] = own[:, 128 * j:128 * (j + 1)]

    def slot(p):
        o = ORDERS[p]
        return ((core * 4 + me[o[2]]) * 4 + me[o[1]]) * 4 + me[o[0]]

    for p, (r0, n) in enumerate(PIECES):
        bufs[p][slot(p)] = head32[r0:r0 + n, :].astype(BF)

    hot = (lax.broadcasted_iota(jnp.int32, (node_ref.shape[0], 128), 0) == lists[...]).astype(F32).astype(BF)
    bound[...] = lax.dot_general(
        hot, node_ref[...], (((0,), (0,)), ((), ())), preferred_element_type=F32).astype(BF)

    pl.semaphore_wait(barrier, len(partners))

    def block(p, step):
        return (core * 4 + lax.rem(me[ORDERS[p][2]] + 4 - step, 4)) * 16

    def send(p, first, size, to, k):
        part = bufs[p].at[pl.ds(first, size)]
        return pltpu.make_async_remote_copy(
            src_ref=part, dst_ref=part, send_sem=send_sem.at[p, k], recv_sem=recv_sem.at[p, k],
            device_id=to, device_id_type=MESH)

    started = []

    def go(copy):
        copy.start()
        started.append(copy)
        return copy

    def spread(p, stage):
        size = 4 ** stage
        first = slot(p) // size * size
        return [go(send(p, first, size, peer(ORDERS[p][stage], s), 3 * stage + s - 1)) for s in (2, 1, 3)]

    def across(p, first, size, k):
        return go(send(p, first, size, sibling, k))

    def arrived(copies):
        for c in copies:
            c.wait_recv()

    one = [spread(p, 0) for p in range(3)]
    halos = []
    for k, to in enumerate(halo_to):
        halos.append(go(pltpu.make_async_remote_copy(
            src_ref=bound, dst_ref=halo.at[pl.ds(128 * k, 128)], send_sem=hsend_sem.at[k], recv_sem=hrecv_sem.at[k],
            device_id=to, device_id_type=MESH)))
    two = []
    for p in range(3):
        arrived(one[p])
        two.append(spread(p, 1))
    right, left, cross = [], [], []
    for p in range(3):
        arrived(two[p])
        ax = ORDERS[p][2]
        right.append(go(send(p, block(p, 0), 16, peer(ax, 1), 6)))
        left.append(go(send(p, block(p, 0), 16, peer(ax, 3), 7)))
    for p in range(3):
        cross.append(across(p, block(p, 0), 16, 10))
    far = []
    for p in range(3):
        ax = ORDERS[p][2]
        right[p].wait_recv()
        far.append(go(send(p, block(p, 1), 8, peer(ax, 1), 8)))
        left[p].wait_recv()
        far.append(go(send(p, block(p, 3) + 8, 8, peer(ax, 3), 9)))
        cross.append(across(p, block(p, 1), 16, 11))
        cross.append(across(p, block(p, 3), 16, 12))
    for p in range(3):
        arrived(far[2 * p:2 * p + 2])
        cross.append(across(p, block(p, 2), 16, 13))
    arrived(cross)

    @pl.loop(0, 128)
    def _(q):
        c, u, v, w = q // 64, lax.rem(q // 16, 4), lax.rem(q // 4, 4), lax.rem(q, 4)
        for p, (r0, n) in enumerate(PIECES):
            pos = {ORDERS[p][2]: u, ORDERS[p][1]: v, ORDERS[p][0]: w}
            aa, bb = device_at(c, pos[1], pos[2], pos[3])
            table[pl.ds((aa * 32 + bb) * NCD + r0 // 4, n // 4)] = bufs[p][q].astype(F32).reshape(n // 4, 4, 128)

    ce = cedges.shape[0]
    for e in range(ce):
        rows_s[pl.ds(4 * e, 4), :] = table[csnd[e]]
        rows_r[pl.ds(4 * e, 4), :] = table[crcv[e]]
    x = cedges[...]
    take = lambda ref: jnp.concatenate([ref[pl.ds(j, ce, stride=4), :] for j in range(4)], 1).astype(BF)
    pre = (
        jnp.dot(x, w1[0:512, :], preferred_element_type=F32)
        + jnp.dot(take(rows_s), w1[512:1024, :], preferred_element_type=F32)
        + jnp.dot(take(rows_r), w1[1024:1536, :], preferred_element_type=F32)
        + b1[...]
    )
    y = jnp.dot(silu(pre).astype(BF), w2[...], preferred_element_type=F32) + b2[...]
    m = norm_rows(y, gain[...], shift[...])
    new_coarse[...] = (x.astype(F32) + m).astype(BF)
    mb = m.astype(BF)

    c = crow[...]
    owner = lax.shift_right_logical(c * 52429, 20)
    local = c - owner * NCD
    iota = lambda shape, d: lax.broadcasted_iota(jnp.int32, shape, d)
    own_hot = (iota((128, ce), 0) == owner).astype(F32)
    before = (iota((ce, ce), 0) < iota((ce, ce), 1)).astype(F32).astype(BF)
    counts = jnp.dot(own_hot.astype(BF), before, preferred_element_type=F32)
    rank = jnp.sum(own_hot * counts, axis=0, keepdims=True)
    for s in range(3):
        placed = jnp.where(rank == s, own_hot, 0.0).astype(BF)
        got = jnp.dot(placed, mb, preferred_element_type=F32)
        for j in range(4):
            wide[pl.ds(4 * s + j, 128, stride=16), :] = got[:, 128 * j:128 * (j + 1)]
    tags = (iota((128, ce), 0).astype(F32) == rank * 32.0 + local.astype(F32)).astype(F32).astype(BF)
    wide[pl.ds(12, 128, stride=16), :] = lax.dot_general(
        own_hot.astype(BF), tags, (((1,), (1,)), ((), ())), preferred_element_type=F32)
    for j in range(1, 4):
        wide[pl.ds(12 + j, 128, stride=16), :] = jnp.zeros((128, 128), F32)
    outbound[...] = wide[...].astype(BF)

    for h in halos:
        h.wait_recv()
    for k in started:
        k.wait_send()


def comm_call(nodes, lists, cedges, csnd, crcv, w1, b1, w2, b2, gain, shift):
    D = 512
    row = lambda v: v.reshape(1, -1)
    vm = pl.BlockSpec(memory_space=pltpu.VMEM)
    sm = pl.BlockSpec(memory_space=pltpu.SMEM)
    ce = cedges.shape[0]
    return pl.pallas_call(
        comm_kernel,
        out_shape=(
            jax.ShapeDtypeStruct((512, D), BF),
            jax.ShapeDtypeStruct((ce, D), BF),
            jax.ShapeDtypeStruct((2048, 128), BF),
        ),
        in_specs=[sm, sm] + [vm] * 10,
        out_specs=(vm, vm, vm),
        scratch_shapes=[
            pltpu.VMEM((128, 32, 128), BF), pltpu.VMEM((128, 32, 128), BF), pltpu.VMEM((128, 16, 128), BF),
            pltpu.VMEM((128 * NCD, 4, 128), F32),
            pltpu.VMEM((ce * 4, 128), F32), pltpu.VMEM((ce * 4, 128), F32),
            pltpu.VMEM((2048, 128), F32),
            pltpu.VMEM((128, D), BF),
            pltpu.VMEM((128, 128), F32),
            pltpu.SemaphoreType.DMA((3, 14)), pltpu.SemaphoreType.DMA((3, 14)),
            pltpu.SemaphoreType.DMA((4,)), pltpu.SemaphoreType.DMA((4,)),
        ],
        compiler_params=pltpu.CompilerParams(
            collective_id=0, has_side_effects=True, vmem_limit_bytes=60 * 2**20),
        cost_estimate=pl.CostEstimate(flops=10**9, bytes_accessed=8 * 10**6, transcendentals=10**5),
        name="coarse",
    )(csnd, crcv, nodes, row(lists), cedges, row(crcv), w1, row(b1), w2, row(b2), row(gain), row(shift))


def tail_kernel(node_ref, head, inbound, w1, b1, w2, b2, gain, shift, _, out, wide):
    wide[...] = inbound[...].astype(F32)
    tags = wide[pl.ds(12, 128, stride=16), :].astype(BF)
    total = head[...]
    for s in range(3):
        got = jnp.concatenate([wide[pl.ds(4 * s + j, 128, stride=16), :] for j in range(4)], 1).astype(BF)
        total = total + lax.dot_general(
            tags[:, 32 * s:32 * s + 32], got, (((0,), (0,)), ((), ())), preferred_element_type=F32)
    rows = node_ref[...]
    pre = (
        jnp.dot(rows, w1[0:512, :], preferred_element_type=F32)
        + jnp.dot(total.astype(BF), w1[512:1024, :], preferred_element_type=F32)
        + b1[...]
    )
    y = jnp.dot(silu(pre).astype(BF), w2[...], preferred_element_type=F32) + b2[...]
    out[...] = (rows.astype(F32) + norm_rows(y, gain[...], shift[...])).astype(BF)


def tail_call(nodes, head, inbound, w1, b1, w2, b2, gain, shift, new_nodes):
    D = 512
    row = lambda v: v.reshape(1, D)
    full = lambda s: pl.BlockSpec(s, lambda i: (0,) * len(s))
    return pl.pallas_call(
        tail_kernel,
        out_shape=jax.ShapeDtypeStruct(new_nodes.shape, BF),
        grid=(1,),
        in_specs=[full((32, D)), full((32, D)), full((2048, 128)), full((2 * D, D)), full((1, D)), full((D, D)),
                  full((1, D)), full((1, D)), full((1, D)), pl.BlockSpec(memory_space=pl.ANY)],
        out_specs=full((32, D)),
        scratch_shapes=[pltpu.VMEM((2048, 128), F32)],
        input_output_aliases={9: 0},
        compiler_params=pltpu.CompilerParams(vmem_limit_bytes=48 * 2**20),
        cost_estimate=pl.CostEstimate(flops=10**8, bytes_accessed=3 * 10**6, transcendentals=10**4),
        name="tail",
    )(nodes, head, inbound, w1, row(b1), w2, row(b2), row(gain), row(shift), new_nodes)


AXES = ("gx", "gy")


def on_device(
    node_feats, edge_feats, senders, receivers, send_lists, coarse_edges, coarse_senders, coarse_receivers,
    edge_w1, edge_b1, edge_w2, edge_b2, edge_gain, edge_shift,
    node_w1, node_b1, node_w2, node_b2, node_gain, node_shift,
):
    halo, new_coarse, outbound = comm_call(
        node_feats, send_lists, coarse_edges, coarse_senders, coarse_receivers,
        edge_w1, edge_b1, edge_w2, edge_b2, edge_gain, edge_shift)
    inbound = lax.all_to_all(outbound.reshape(128, 16, 128), AXES, 0, 0, tiled=True).reshape(2048, 128)
    new_edges, new_nodes, head = fine_call(
        senders, receivers, edge_feats, node_feats, halo,
        edge_w1, edge_b1, edge_w2, edge_b2, edge_gain, edge_shift,
        node_w1, node_b1, node_w2, node_b2, node_gain, node_shift)
    new_nodes = tail_call(
        node_feats, head, inbound, node_w1, node_b1, node_w2, node_b2, node_gain, node_shift, new_nodes)
    return new_nodes, new_edges, new_coarse


def solution(mesh):
    rows, flat, rep = P(AXES, None), P(AXES), P()
    return jax.shard_map(
        on_device, mesh=mesh,
        in_specs=(rows, rows, flat, flat, flat, rows, flat, flat) + (rep,) * 12,
        out_specs=(rows, rows, rows), check_vma=False,
    )
```

```python
import functools
import jax
import jax.numpy as jnp
from jax import lax
from jax.experimental import pallas as pl
from jax.experimental.pallas import tpu as pltpu
from jax.sharding import PartitionSpec as P

BF, F32 = jnp.bfloat16, jnp.float32
MESH = pl.DeviceIdType.MESH
D = 512
NCD = 20
BLK = 256
WIN = 264
PIECES = ((0, 32), (32, 32), (64, 16))
ORDERS = ((3, 2, 1), (2, 1, 3), (1, 3, 2))
SEGMENTS = ((0, 1), (1, 2), (2, 3), (3, 4), (4, 8))


def norm_rows(x, gain, shift):
    mean = jnp.mean(x, -1, keepdims=True)
    c = x - mean
    var = jnp.mean(c * c, -1, keepdims=True)
    return c * lax.rsqrt(var + 1e-05) * gain + shift


def silu(x):
    t = 0.5 * x
    return t + t * jnp.tanh(t)


def iota(shape, dim):
    return lax.broadcasted_iota(jnp.int32, shape, dim)


def coords(a, b):
    return lax.rem(a, 2), (a // 2) * 2 + b // 16, lax.rem(b // 4, 4), lax.rem(b, 4)


def device_at(core, z, x, y):
    return ((z // 2) * 2 + core, lax.rem(z, 2) * 16 + x * 4 + y)


def edge_kernel(
    snd, rcv, csnd, crcv,
    node_ref, lists, edges_in, cedges, crow, w1, b1, w2, b2, gain, shift,
    edges_out, msg_out, new_coarse, inbound,
    edges, new_edges, msg, p_snd, p_rcv, g_a, g_b,
    buf0, buf1, buf2, table, rows_s, rows_r, wide, outb, bound, halo, head32,
    send_sem, recv_sem, hsend_sem, hrecv_sem, out_send, in_recv, load_sem, store_sem,
):
    a, b = lax.axis_index("gx"), lax.axis_index("gy")
    me = coords(a, b)
    core = me[0]
    bufs = (buf0, buf1, buf2)
    nodes = node_ref.shape[0]

    load = pltpu.make_async_copy(edges_in, edges, load_sem)
    load.start()

    def peer(axis, step):
        c = list(me)
        c[axis] = lax.rem(c[axis] + step, 4)
        return device_at(*c)

    sibling = (a + 1 - 2 * core, b)
    halo_to = (
        (lax.rem(a + 1, 4), b), (lax.rem(a + 3, 4), b),
        (a, lax.rem(b + 1, 32)), (a, lax.rem(b + 31, 32)),
    )
    partners = [peer(axis, s) for axis in (1, 2, 3) for s in (1, 2, 3)] + [sibling] + list(halo_to)
    barrier = pltpu.get_barrier_semaphore()
    for p in partners:
        pl.semaphore_signal(barrier, inc=1, device_id=p, device_id_type=MESH)

    own = node_ref[0:32, :].astype(F32)
    for j in range(4):
        head32[pl.ds(j, 32, stride=4), :] = own[:, 128 * j:128 * (j + 1)]

    def slot(p):
        o = ORDERS[p]
        return ((core * 4 + me[o[2]]) * 4 + me[o[1]]) * 4 + me[o[0]]

    for p, (r0, n) in enumerate(PIECES):
        bufs[p][slot(p)] = head32[r0:r0 + n, :].astype(BF)

    hot = (iota((nodes, 128), 0) == lists[...]).astype(F32).astype(BF)
    bound[...] = lax.dot_general(
        hot, node_ref[...], (((0,), (0,)), ((), ())), preferred_element_type=F32).astype(BF)

    def block(p, step):
        return (core * 4 + lax.rem(me[ORDERS[p][2]] + 4 - step, 4)) * 16

    def send(p, first, size, to, k):
        part = bufs[p].at[pl.ds(first, size)]
        return pltpu.make_async_remote_copy(
            src_ref=part, dst_ref=part, send_sem=send_sem.at[p, k], recv_sem=recv_sem.at[p, k],
            device_id=to, device_id_type=MESH)

    started = []

    def go(copy):
        copy.start()
        started.append(copy)
        return copy

    def spread(p, stage):
        size = 4 ** stage
        first = slot(p) // size * size
        return [go(send(p, first, size, peer(ORDERS[p][stage], s), 3 * stage + s - 1)) for s in (2, 1, 3)]

    def across(p, first, size, k):
        return go(send(p, first, size, sibling, k))

    def arrived(copies):
        for c in copies:
            c.wait_recv()

    def project(rows, lo, tab, at, bias):
        n = rows.shape[0]
        v = jnp.dot(rows, w1[lo:lo + 512, :], preferred_element_type=F32)
        if bias is not None:
            v = v + bias
        for j in range(4):
            tab[pl.ds(at, n), j, :] = v[:, 128 * j:128 * (j + 1)]

    def project_own(lo, hi):
        @pl.loop(lo, hi)
        def _(c):
            at = pl.multiple_of(c * 256, 256)
            rows = node_ref[pl.ds(at, 256), :]
            project(rows, 512, p_snd, at, None)
            project(rows, 1024, p_rcv, at, b1[...])

    def gather(k, g):
        base = k * BLK
        for e in range(BLK):
            g[pl.ds(4 * e, 4), :] = p_snd[snd[base + e]] + p_rcv[rcv[base + e]]

    def compute(k, g):
        at = pl.multiple_of(k * BLK, BLK)
        x = edges[pl.ds(at, BLK), :]
        pre = jnp.dot(x, w1[0:512, :], preferred_element_type=F32)
        pre = pre + jnp.concatenate([g[pl.ds(j, BLK, stride=4), :] for j in range(4)], 1)
        y = jnp.dot(silu(pre).astype(BF), w2[...], preferred_element_type=F32) + b2[...]
        m = norm_rows(y, gain[...], shift[...])
        new_edges[pl.ds(at, BLK), :] = (x.astype(F32) + m).astype(BF)
        msg[pl.ds(at, BLK), :] = m.astype(BF)

    last = edges.shape[0] // BLK - 1

    def stores(i):
        part = pl.ds(pl.multiple_of(i * 2 * BLK, 2 * BLK), 2 * BLK)
        return (
            pltpu.make_async_copy(new_edges.at[part], edges_out.at[part], store_sem.at[0, i]),
            pltpu.make_async_copy(msg.at[part], msg_out.at[part], store_sem.at[1, i]),
        )

    def pairs(lo, hi):
        @pl.loop(lo, hi)
        def _(i):
            gather(2 * i + 1, g_b)
            compute(2 * i, g_a)
            gather(jnp.minimum(2 * i + 2, last), g_a)
            compute(2 * i + 1, g_b)
            for c in stores(i):
                c.start()

    project_own(0, nodes // 256)
    pl.semaphore_wait(barrier, len(partners))
    one = [spread(p, 0) for p in range(3)]
    halos = []
    for k, to in enumerate(halo_to):
        halos.append(go(pltpu.make_async_remote_copy(
            src_ref=bound, dst_ref=halo.at[pl.ds(128 * k, 128)], send_sem=hsend_sem.at[k], recv_sem=hrecv_sem.at[k],
            device_id=to, device_id_type=MESH)))
    two = []
    for p in range(3):
        arrived(one[p])
        two.append(spread(p, 1))
    for k in range(4):
        halos[k].wait_recv()
    for k in range(2):
        project(halo[256 * k:256 * (k + 1), :], 512, p_snd, nodes + 256 * k, None)
    load.wait()
    gather(0, g_a)
    pairs(*SEGMENTS[0])
    right, left, cross = [], [], []
    for p in range(3):
        arrived(two[p])
        ax = ORDERS[p][2]
        right.append(go(send(p, block(p, 0), 16, peer(ax, 1), 6)))
        left.append(go(send(p, block(p, 0), 16, peer(ax, 3), 7)))
    for p in range(3):
        cross.append(across(p, block(p, 0), 16, 10))
    pairs(*SEGMENTS[1])
    far = []
    for p in range(3):
        ax = ORDERS[p][2]
        right[p].wait_recv()
        far.append(go(send(p, block(p, 1), 8, peer(ax, 1), 8)))
        left[p].wait_recv()
        far.append(go(send(p, block(p, 3) + 8, 8, peer(ax, 3), 9)))
        cross.append(across(p, block(p, 1), 16, 11))
        cross.append(across(p, block(p, 3), 16, 12))
    pairs(*SEGMENTS[2])
    for p in range(3):
        arrived(far[2 * p:2 * p + 2])
        cross.append(across(p, block(p, 2), 16, 13))
    pairs(*SEGMENTS[3])
    arrived(cross)

    @pl.loop(0, 128)
    def _(q):
        c, u, v, w = q // 64, lax.rem(q // 16, 4), lax.rem(q // 4, 4), lax.rem(q, 4)
        for p, (r0, n) in enumerate(PIECES):
            pos = {ORDERS[p][2]: u, ORDERS[p][1]: v, ORDERS[p][0]: w}
            aa, bb = device_at(c, pos[1], pos[2], pos[3])
            table[pl.ds((aa * 32 + bb) * NCD + r0 // 4, n // 4)] = bufs[p][q].astype(F32).reshape(n // 4, 4, 128)

    ce = cedges.shape[0]
    for e in range(ce):
        rows_s[pl.ds(4 * e, 4), :] = table[csnd[e]]
        rows_r[pl.ds(4 * e, 4), :] = table[crcv[e]]
    x = cedges[...]
    take = lambda ref: jnp.concatenate([ref[pl.ds(j, ce, stride=4), :] for j in range(4)], 1).astype(BF)
    pre = (
        jnp.dot(x, w1[0:512, :], preferred_element_type=F32)
        + jnp.dot(take(rows_s), w1[512:1024, :], preferred_element_type=F32)
        + jnp.dot(take(rows_r), w1[1024:1536, :], preferred_element_type=F32)
        + b1[...]
    )
    y = jnp.dot(silu(pre).astype(BF), w2[...], preferred_element_type=F32) + b2[...]
    m = norm_rows(y, gain[...], shift[...])
    new_coarse[...] = (x.astype(F32) + m).astype(BF)
    mb = m.astype(BF)

    c = crow[...]
    owner = lax.shift_right_logical(c * 52429, 20)
    local = c - owner * NCD
    own_hot = (iota((128, ce), 0) == owner).astype(F32)
    before = (iota((ce, ce), 0) < iota((ce, ce), 1)).astype(F32).astype(BF)
    counts = jnp.dot(own_hot.astype(BF), before, preferred_element_type=F32)
    rank = jnp.sum(own_hot * counts, axis=0, keepdims=True)
    for s in range(3):
        placed = jnp.where(rank == s, own_hot, 0.0).astype(BF)
        got = jnp.dot(placed, mb, preferred_element_type=F32)
        for j in range(4):
            wide[pl.ds(4 * s + j, 128, stride=16), :] = got[:, 128 * j:128 * (j + 1)]
    tags = (iota((128, ce), 0).astype(F32) == rank * 32.0 + local.astype(F32)).astype(F32).astype(BF)
    wide[pl.ds(12, 128, stride=16), :] = lax.dot_general(
        own_hot.astype(BF), tags, (((1,), (1,)), ((), ())), preferred_element_type=F32)
    for j in range(1, 4):
        wide[pl.ds(12 + j, 128, stride=16), :] = jnp.zeros((128, 128), F32)
    outb[...] = wide[...].astype(BF).reshape(128, 16, 128)

    g = a * 32 + b
    inbound[0] = outb[g]

    @pl.loop(1, 128)
    def _(k):
        to = lax.rem(g + k, 128)
        pltpu.make_async_remote_copy(
            src_ref=outb.at[to], dst_ref=inbound.at[k], send_sem=out_send, recv_sem=in_recv,
            device_id=(to // 32, lax.rem(to, 32)), device_id_type=MESH).start()

    pairs(*SEGMENTS[4])

    most = pl.ds(1, 127)
    pltpu.make_async_copy(inbound.at[most], inbound.at[most], in_recv).wait()
    pltpu.make_async_copy(outb.at[most], outb.at[most], out_send).wait()
    for k in started:
        k.wait_send()
    for i in range(edges.shape[0] // (2 * BLK)):
        for c in stores(i):
            c.wait()


def edge_call(snd, rcv, csnd, crcv, nodes, lists, edges, cedges, w1, b1, w2, b2, gain, shift):
    row = lambda v: v.reshape(1, -1)
    vm = pl.BlockSpec(memory_space=pltpu.VMEM)
    sm = pl.BlockSpec(memory_space=pltpu.SMEM)
    hbm = pl.BlockSpec(memory_space=pl.ANY)
    ce, E, N = cedges.shape[0], edges.shape[0], nodes.shape[0]
    return pl.pallas_call(
        edge_kernel,
        out_shape=(
            jax.ShapeDtypeStruct((E, D), BF),
            jax.ShapeDtypeStruct((E, D), BF),
            jax.ShapeDtypeStruct((ce, D), BF),
            jax.ShapeDtypeStruct((128, 16, 128), BF),
        ),
        in_specs=[sm] * 4 + [vm, vm, hbm] + [vm] * 8,
        out_specs=(hbm, hbm, vm, vm),
        scratch_shapes=[
            pltpu.VMEM((E, D), BF), pltpu.VMEM((E, D), BF), pltpu.VMEM((E, D), BF),
            pltpu.VMEM((N + 512, 4, 128), F32), pltpu.VMEM((N, 4, 128), F32),
            pltpu.VMEM((BLK * 4, 128), F32), pltpu.VMEM((BLK * 4, 128), F32),
            pltpu.VMEM((128, 32, 128), BF), pltpu.VMEM((128, 32, 128), BF), pltpu.VMEM((128, 16, 128), BF),
            pltpu.VMEM((128 * NCD, 4, 128), F32),
            pltpu.VMEM((ce * 4, 128), F32), pltpu.VMEM((ce * 4, 128), F32),
            pltpu.VMEM((2048, 128), F32), pltpu.VMEM((128, 16, 128), BF),
            pltpu.VMEM((128, D), BF), pltpu.VMEM((512, D), BF), pltpu.VMEM((128, 128), F32),
            pltpu.SemaphoreType.DMA((3, 14)), pltpu.SemaphoreType.DMA((3, 14)),
            pltpu.SemaphoreType.DMA((4,)), pltpu.SemaphoreType.DMA((4,)),
            pltpu.SemaphoreType.DMA, pltpu.SemaphoreType.DMA,
            pltpu.SemaphoreType.DMA, pltpu.SemaphoreType.DMA((2, 8)),
        ],
        compiler_params=pltpu.CompilerParams(
            collective_id=0, has_side_effects=True, vmem_limit_bytes=60 * 2**20),
        cost_estimate=pl.CostEstimate(flops=7 * 10**9, bytes_accessed=2 * 10**7, transcendentals=2 * 10**6),
        name="edges",
    )(snd, rcv, csnd, crcv, nodes, row(lists), edges, cedges, row(crcv), w1, row(b1), w2, row(b2), row(gain), row(shift))


def node_kernel(
    rcv,
    edges_in, msg, rrow, inbound, node_ref, w1, b1, w2, b2, gain, shift,
    edges_out, new_nodes,
    fsum, wide, copy_sem,
    *, esteps,
):
    i = pl.program_id(0)
    keep = pltpu.make_async_copy(edges_in, edges_out, copy_sem)

    @pl.when(i == 0)
    def _():
        keep.start()
        fsum[...] = jnp.zeros_like(fsum)

    @pl.when(i < esteps)
    def _():
        for k in range(2):
            start = pl.multiple_of((rcv[(2 * i + k) * BLK] // 8) * 8, 8)
            ids = rrow[0, k:k + 1, :]
            hot = (ids - start == iota((WIN, BLK), 0)).astype(F32).astype(BF)
            fsum[pl.ds(start, WIN), :] += jnp.dot(hot, msg[pl.ds(k * BLK, BLK), :], preferred_element_type=F32)

    @pl.when(i == esteps)
    def _():
        wide[...] = inbound[...].astype(F32)
        tags = wide[pl.ds(12, 128, stride=16), :].astype(BF)
        total = fsum[0:32, :]
        for s in range(3):
            got = jnp.concatenate([wide[pl.ds(4 * s + j, 128, stride=16), :] for j in range(4)], 1).astype(BF)
            total = total + lax.dot_general(
                tags[:, 32 * s:32 * s + 32], got, (((0,), (0,)), ((), ())), preferred_element_type=F32)
        fsum[0:32, :] = total

    @pl.when(i >= esteps)
    def _():
        at = pl.multiple_of((i - esteps) * 256, 256)
        rows = node_ref[pl.ds(at, 256), :]
        pre = (
            jnp.dot(rows, w1[0:512, :], preferred_element_type=F32)
            + jnp.dot(fsum[pl.ds(at, 256), :].astype(BF), w1[512:1024, :], preferred_element_type=F32)
            + b1[...]
        )
        y = jnp.dot(silu(pre).astype(BF), w2[...], preferred_element_type=F32) + b2[...]
        new_nodes[...] = (rows.astype(F32) + norm_rows(y, gain[...], shift[...])).astype(BF)

    @pl.when(i == pl.num_programs(0) - 1)
    def _():
        keep.wait()


def node_call(rcv, edges, msg, inbound, nodes, w1, b1, w2, b2, gain, shift):
    E, N = msg.shape[0], nodes.shape[0]
    esteps, nsteps = E // (2 * BLK), N // 256
    row = lambda v: v.reshape(1, D)
    full = lambda s: pl.BlockSpec(s, lambda i, *_: (0,) * len(s))
    hbm = pl.BlockSpec(memory_space=pl.ANY)
    return pl.pallas_call(
        functools.partial(node_kernel, esteps=esteps),
        out_shape=(jax.ShapeDtypeStruct((E, D), BF), jax.ShapeDtypeStruct((N, D), BF)),
        grid_spec=pltpu.PrefetchScalarGridSpec(
            num_scalar_prefetch=1,
            grid=(esteps + nsteps,),
            in_specs=[
                hbm,
                pl.BlockSpec((2 * BLK, D), lambda i, *_: (jnp.minimum(i, esteps - 1), 0)),
                pl.BlockSpec((1, 2, BLK), lambda i, *_: (jnp.minimum(i, esteps - 1), 0, 0)),
                full((2048, 128)), full((N, D)),
                full((2 * D, D)), full((1, D)), full((D, D)), full((1, D)), full((1, D)), full((1, D)),
            ],
            out_specs=(hbm, pl.BlockSpec((256, D), lambda i, *_: (jnp.maximum(i - esteps, 0), 0))),
            scratch_shapes=[
                pltpu.VMEM((N + WIN, D), F32), pltpu.VMEM((2048, 128), F32), pltpu.SemaphoreType.DMA,
            ],
        ),
        compiler_params=pltpu.CompilerParams(vmem_limit_bytes=60 * 2**20, dimension_semantics=("arbitrary",)),
        cost_estimate=pl.CostEstimate(flops=3 * 10**9, bytes_accessed=16 * 10**6, transcendentals=10**6),
        name="nodes",
    )(rcv, edges, msg, rcv.reshape(esteps, 2, BLK), inbound.reshape(2048, 128), nodes,
      w1, row(b1), w2, row(b2), row(gain), row(shift))


AXES = ("gx", "gy")


def on_device(
    node_feats, edge_feats, senders, receivers, send_lists, coarse_edges, coarse_senders, coarse_receivers,
    edge_w1, edge_b1, edge_w2, edge_b2, edge_gain, edge_shift,
    node_w1, node_b1, node_w2, node_b2, node_gain, node_shift,
):
    new_edges, message, new_coarse, inbound = edge_call(
        senders, receivers, coarse_senders, coarse_receivers, node_feats, send_lists, edge_feats, coarse_edges,
        edge_w1, edge_b1, edge_w2, edge_b2, edge_gain, edge_shift)
    new_edges, new_nodes = node_call(
        receivers, new_edges, message, inbound, node_feats,
        node_w1, node_b1, node_w2, node_b2, node_gain, node_shift)
    return new_nodes, new_edges, new_coarse


def solution(mesh):
    rows, flat, rep = P(AXES, None), P(AXES), P()
    return jax.shard_map(
        on_device, mesh=mesh,
        in_specs=(rows, rows, flat, flat, flat, rows, flat, flat) + (rep,) * 12,
        out_specs=(rows, rows, rows), check_vma=False,
    )
```

```python
import functools
import jax
import jax.numpy as jnp
from jax import lax
from jax.experimental import pallas as pl
from jax.experimental.pallas import tpu as pltpu
from jax.sharding import PartitionSpec as P

BF, F32 = jnp.bfloat16, jnp.float32
MESH = pl.DeviceIdType.MESH
D = 512
NCD = 20
BLK = 256
WIN = 264
PIECES = ((0, 32), (32, 32), (64, 16))
ORDERS = ((3, 2, 1), (2, 1, 3), (1, 3, 2))
SEGMENTS = ((0, 1), (1, 2), (2, 3), (3, 3), (3, 4), (4, 8))


def norm_rows(x, gain, shift):
    mean = jnp.mean(x, -1, keepdims=True)
    c = x - mean
    var = jnp.mean(c * c, -1, keepdims=True)
    return c * lax.rsqrt(var + 1e-05) * gain + shift


def silu(x):
    t = 0.5 * x
    return t + t * jnp.tanh(t)


def iota(shape, dim):
    return lax.broadcasted_iota(jnp.int32, shape, dim)


def coords(a, b):
    return lax.rem(a, 2), (a // 2) * 2 + b // 16, lax.rem(b // 4, 4), lax.rem(b, 4)


def device_at(core, z, x, y):
    return ((z // 2) * 2 + core, lax.rem(z, 2) * 16 + x * 4 + y)


def edge_kernel(
    snd, rcv, csnd, crcv,
    node_ref, lists, edges_in, cedges, crow, w1, b1, w2, b2, gain, shift,
    edges_out, msg_out, new_coarse, inbound,
    edges, new_edges, msg, p_snd, p_rcv, g_a, g_b,
    buf0, buf1, buf2, table, rows_s, rows_r, wide, outb, bound, halo, head32,
    send_sem, recv_sem, hsend_sem, hrecv_sem, out_send, in_recv, load_sem, store_sem,
):
    a, b = lax.axis_index("gx"), lax.axis_index("gy")
    me = coords(a, b)
    core = me[0]
    bufs = (buf0, buf1, buf2)
    nodes = node_ref.shape[0]

    load = pltpu.make_async_copy(edges_in, edges, load_sem)
    load.start()

    def peer(axis, step):
        c = list(me)
        c[axis] = lax.rem(c[axis] + step, 4)
        return device_at(*c)

    sibling = (a + 1 - 2 * core, b)
    halo_to = (
        (lax.rem(a + 1, 4), b), (lax.rem(a + 3, 4), b),
        (a, lax.rem(b + 1, 32)), (a, lax.rem(b + 31, 32)),
    )
    partners = [peer(axis, s) for axis in (1, 2, 3) for s in (1, 2, 3)] + [sibling] + list(halo_to)
    barrier = pltpu.get_barrier_semaphore()
    for p in partners:
        pl.semaphore_signal(barrier, inc=1, device_id=p, device_id_type=MESH)

    own = node_ref[0:32, :].astype(F32)
    for j in range(4):
        head32[pl.ds(j, 32, stride=4), :] = own[:, 128 * j:128 * (j + 1)]

    def slot(p):
        o = ORDERS[p]
        return ((core * 4 + me[o[2]]) * 4 + me[o[1]]) * 4 + me[o[0]]

    for p, (r0, n) in enumerate(PIECES):
        bufs[p][slot(p)] = head32[r0:r0 + n, :].astype(BF)

    hot = (iota((nodes, 128), 0) == lists[...]).astype(F32).astype(BF)
    bound[...] = lax.dot_general(
        hot, node_ref[...], (((0,), (0,)), ((), ())), preferred_element_type=F32).astype(BF)

    def block(p, step):
        return (core * 4 + lax.rem(me[ORDERS[p][2]] + 4 - step, 4)) * 16

    def send(p, first, size, to, k):
        part = bufs[p].at[pl.ds(first, size)]
        return pltpu.make_async_remote_copy(
            src_ref=part, dst_ref=part, send_sem=send_sem.at[p, k], recv_sem=recv_sem.at[p, k],
            device_id=to, device_id_type=MESH)

    started = []

    def go(copy):
        copy.start()
        started.append(copy)
        return copy

    def spread(p, stage):
        size = 4 ** stage
        first = slot(p) // size * size
        return [go(send(p, first, size, peer(ORDERS[p][stage], s), 3 * stage + s - 1)) for s in (2, 1, 3)]

    def across(p, first, size, k):
        return go(send(p, first, size, sibling, k))

    def arrived(copies):
        for c in copies:
            c.wait_recv()

    def project(rows, lo, tab, at, bias):
        n = rows.shape[0]
        v = jnp.dot(rows, w1[lo:lo + 512, :], preferred_element_type=F32)
        if bias is not None:
            v = v + bias
        for j in range(4):
            tab[pl.ds(at, n), j, :] = v[:, 128 * j:128 * (j + 1)]

    def project_own(lo, hi):
        @pl.loop(lo, hi)
        def _(c):
            at = pl.multiple_of(c * 256, 256)
            rows = node_ref[pl.ds(at, 256), :]
            project(rows, 512, p_snd, at, None)
            project(rows, 1024, p_rcv, at, b1[...])

    def gather(k, g):
        base = k * BLK
        for e in range(BLK):
            g[pl.ds(4 * e, 4), :] = p_snd[snd[base + e]] + p_rcv[rcv[base + e]]

    def compute(k, g):
        at = pl.multiple_of(k * BLK, BLK)
        x = edges[pl.ds(at, BLK), :]
        pre = jnp.dot(x, w1[0:512, :], preferred_element_type=F32)
        pre = pre + jnp.concatenate([g[pl.ds(j, BLK, stride=4), :] for j in range(4)], 1)
        y = jnp.dot(silu(pre).astype(BF), w2[...], preferred_element_type=F32) + b2[...]
        m = norm_rows(y, gain[...], shift[...])
        new_edges[pl.ds(at, BLK), :] = (x.astype(F32) + m).astype(BF)
        msg[pl.ds(at, BLK), :] = m.astype(BF)

    last = edges.shape[0] // BLK - 1

    def stores(i):
        part = pl.ds(pl.multiple_of(i * 2 * BLK, 2 * BLK), 2 * BLK)
        return (
            pltpu.make_async_copy(new_edges.at[part], edges_out.at[part], store_sem.at[0, i]),
            pltpu.make_async_copy(msg.at[part], msg_out.at[part], store_sem.at[1, i]),
        )

    def pairs(lo, hi):
        @pl.loop(lo, hi)
        def _(i):
            gather(2 * i + 1, g_b)
            compute(2 * i, g_a)
            gather(jnp.minimum(2 * i + 2, last), g_a)
            compute(2 * i + 1, g_b)
            for c in stores(i):
                c.start()

    def fill(c):
        @pl.loop(0, 64)
        def _(q):
            u, v, w = q // 16, lax.rem(q // 4, 4), lax.rem(q, 4)
            for p, (r0, n) in enumerate(PIECES):
                pos = {ORDERS[p][2]: u, ORDERS[p][1]: v, ORDERS[p][0]: w}
                aa, bb = device_at(c, pos[1], pos[2], pos[3])
                table[pl.ds((aa * 32 + bb) * NCD + r0 // 4, n // 4)] = (
                    bufs[p][c * 64 + q].astype(F32).reshape(n // 4, 4, 128))

    pl.semaphore_wait(barrier, len(partners))
    one = [spread(p, 0) for p in range(3)]
    halos = []
    for k, to in enumerate(halo_to):
        halos.append(go(pltpu.make_async_remote_copy(
            src_ref=bound, dst_ref=halo.at[pl.ds(128 * k, 128)], send_sem=hsend_sem.at[k], recv_sem=hrecv_sem.at[k],
            device_id=to, device_id_type=MESH)))
    project_own(0, nodes // 256)
    two = []
    for p in range(3):
        arrived(one[p])
        two.append(spread(p, 1))
    for k in range(4):
        halos[k].wait_recv()
    for k in range(2):
        project(halo[256 * k:256 * (k + 1), :], 512, p_snd, nodes + 256 * k, None)
    load.wait()
    gather(0, g_a)
    pairs(*SEGMENTS[0])
    three, cross = [], []
    for p in range(3):
        arrived(two[p])
        three.append(spread(p, 2))
    for p in range(3):
        cross.append(across(p, block(p, 0), 16, 10))
    pairs(*SEGMENTS[1])
    for i, s in enumerate((2, 1, 3)):
        for p in range(3):
            three[p][i].wait_recv()
            cross.append(across(p, block(p, s), 16, 10 + s))
        if i < 2:
            pairs(*SEGMENTS[2 + i])
    fill(core)
    pairs(*SEGMENTS[4])
    arrived(cross)
    fill(1 - core)

    ce = cedges.shape[0]
    for e in range(ce):
        rows_s[pl.ds(4 * e, 4), :] = table[csnd[e]]
        rows_r[pl.ds(4 * e, 4), :] = table[crcv[e]]
    x = cedges[...]
    take = lambda ref: jnp.concatenate([ref[pl.ds(j, ce, stride=4), :] for j in range(4)], 1).astype(BF)
    pre = (
        jnp.dot(x, w1[0:512, :], preferred_element_type=F32)
        + jnp.dot(take(rows_s), w1[512:1024, :], preferred_element_type=F32)
        + jnp.dot(take(rows_r), w1[1024:1536, :], preferred_element_type=F32)
        + b1[...]
    )
    y = jnp.dot(silu(pre).astype(BF), w2[...], preferred_element_type=F32) + b2[...]
    m = norm_rows(y, gain[...], shift[...])
    new_coarse[...] = (x.astype(F32) + m).astype(BF)
    mb = m.astype(BF)

    c = crow[...]
    owner = lax.shift_right_logical(c * 52429, 20)
    local = c - owner * NCD
    own_hot = (iota((128, ce), 0) == owner).astype(F32)
    before = (iota((ce, ce), 0) < iota((ce, ce), 1)).astype(F32).astype(BF)
    counts = jnp.dot(own_hot.astype(BF), before, preferred_element_type=F32)
    rank = jnp.sum(own_hot * counts, axis=0, keepdims=True)
    for s in range(3):
        placed = jnp.where(rank == s, own_hot, 0.0).astype(BF)
        got = jnp.dot(placed, mb, preferred_element_type=F32)
        for j in range(4):
            wide[pl.ds(4 * s + j, 128, stride=16), :] = got[:, 128 * j:128 * (j + 1)]
    tags = (iota((128, ce), 0).astype(F32) == rank * 32.0 + local.astype(F32)).astype(F32).astype(BF)
    wide[pl.ds(12, 128, stride=16), :] = lax.dot_general(
        own_hot.astype(BF), tags, (((1,), (1,)), ((), ())), preferred_element_type=F32)
    for j in range(1, 4):
        wide[pl.ds(12 + j, 128, stride=16), :] = jnp.zeros((128, 128), F32)
    outb[...] = wide[...].astype(BF).reshape(128, 16, 128)

    g = a * 32 + b
    inbound[0] = outb[g]

    @pl.loop(1, 128)
    def _(k):
        to = lax.rem(g + k, 128)
        pltpu.make_async_remote_copy(
            src_ref=outb.at[to], dst_ref=inbound.at[k], send_sem=out_send, recv_sem=in_recv,
            device_id=(to // 32, lax.rem(to, 32)), device_id_type=MESH).start()

    pairs(*SEGMENTS[5])

    most = pl.ds(1, 127)
    pltpu.make_async_copy(inbound.at[most], inbound.at[most], in_recv).wait()
    pltpu.make_async_copy(outb.at[most], outb.at[most], out_send).wait()
    for k in started:
        k.wait_send()
    for i in range(edges.shape[0] // (2 * BLK)):
        for c in stores(i):
            c.wait()


def edge_call(snd, rcv, csnd, crcv, nodes, lists, edges, cedges, w1, b1, w2, b2, gain, shift):
    row = lambda v: v.reshape(1, -1)
    vm = pl.BlockSpec(memory_space=pltpu.VMEM)
    sm = pl.BlockSpec(memory_space=pltpu.SMEM)
    hbm = pl.BlockSpec(memory_space=pl.ANY)
    ce, E, N = cedges.shape[0], edges.shape[0], nodes.shape[0]
    return pl.pallas_call(
        edge_kernel,
        out_shape=(
            jax.ShapeDtypeStruct((E, D), BF),
            jax.ShapeDtypeStruct((E, D), BF),
            jax.ShapeDtypeStruct((ce, D), BF),
            jax.ShapeDtypeStruct((128, 16, 128), BF),
        ),
        in_specs=[sm] * 4 + [vm, vm, hbm] + [vm] * 8,
        out_specs=(hbm, hbm, vm, vm),
        scratch_shapes=[
            pltpu.VMEM((E, D), BF), pltpu.VMEM((E, D), BF), pltpu.VMEM((E, D), BF),
            pltpu.VMEM((N + 512, 4, 128), F32), pltpu.VMEM((N, 4, 128), F32),
            pltpu.VMEM((BLK * 4, 128), F32), pltpu.VMEM((BLK * 4, 128), F32),
            pltpu.VMEM((128, 32, 128), BF), pltpu.VMEM((128, 32, 128), BF), pltpu.VMEM((128, 16, 128), BF),
            pltpu.VMEM((128 * NCD, 4, 128), F32),
            pltpu.VMEM((ce * 4, 128), F32), pltpu.VMEM((ce * 4, 128), F32),
            pltpu.VMEM((2048, 128), F32), pltpu.VMEM((128, 16, 128), BF),
            pltpu.VMEM((128, D), BF), pltpu.VMEM((512, D), BF), pltpu.VMEM((128, 128), F32),
            pltpu.SemaphoreType.DMA((3, 14)), pltpu.SemaphoreType.DMA((3, 14)),
            pltpu.SemaphoreType.DMA((4,)), pltpu.SemaphoreType.DMA((4,)),
            pltpu.SemaphoreType.DMA, pltpu.SemaphoreType.DMA,
            pltpu.SemaphoreType.DMA, pltpu.SemaphoreType.DMA((2, 8)),
        ],
        compiler_params=pltpu.CompilerParams(
            collective_id=0, has_side_effects=True, vmem_limit_bytes=60 * 2**20),
        cost_estimate=pl.CostEstimate(flops=7 * 10**9, bytes_accessed=2 * 10**7, transcendentals=2 * 10**6),
        name="edges",
    )(snd, rcv, csnd, crcv, nodes, row(lists), edges, cedges, row(crcv), w1, row(b1), w2, row(b2), row(gain), row(shift))


def node_kernel(
    rcv,
    rrow, edges_in, msg_in, coarse_in, inbound_in, nodes_in, w1_in, w2_in, b1, b2, gain, shift,
    edges_out, coarse_out, nodes_out,
    edges, msg, coarse, inbound, node_ref, w1, w2, new_nodes, fsum, wide,
    msg_sem, edge_sem, back_sem, small_sem, node_sem,
):
    steps, nsteps = msg.shape[0] // (2 * BLK), node_ref.shape[0] // BLK
    part = lambda i: pl.ds(2 * BLK * i, 2 * BLK)
    loads = [pltpu.make_async_copy(msg_in.at[part(i)], msg.at[part(i)], msg_sem.at[i]) for i in range(steps)]
    small = [
        pltpu.make_async_copy(src, dst, small_sem.at[k]) for k, (src, dst) in enumerate((
            (inbound_in, inbound), (nodes_in, node_ref), (w1_in, w1), (w2_in, w2), (coarse_in, coarse)))
    ]
    there = [pltpu.make_async_copy(edges_in.at[part(i)], edges.at[part(i)], edge_sem.at[i]) for i in range(steps)]
    back = [pltpu.make_async_copy(edges.at[part(i)], edges_out.at[part(i)], back_sem.at[i]) for i in range(steps)]
    back.append(pltpu.make_async_copy(coarse, coarse_out, back_sem.at[steps]))
    for c in loads + small + there:
        c.start()
    fsum[...] = jnp.zeros_like(fsum)
    for i in range(steps):
        loads[i].wait()
        for k in (2 * i, 2 * i + 1):
            start = pl.multiple_of((rcv[k * BLK] // 8) * 8, 8)
            ids = rrow[:, k * BLK:(k + 1) * BLK]
            hot = (ids - start == iota((WIN, BLK), 0)).astype(F32).astype(BF)
            fsum[pl.ds(start, WIN), :] += jnp.dot(hot, msg[k * BLK:(k + 1) * BLK, :], preferred_element_type=F32)
    for c in small:
        c.wait()
    back[steps].start()
    for i in range(steps):
        there[i].wait()
        back[i].start()

    wide[...] = inbound[...].astype(F32)
    tags = wide[pl.ds(12, 128, stride=16), :].astype(BF)
    total = fsum[0:32, :]
    for s in range(3):
        got = jnp.concatenate([wide[pl.ds(4 * s + j, 128, stride=16), :] for j in range(4)], 1).astype(BF)
        total = total + lax.dot_general(
            tags[:, 32 * s:32 * s + 32], got, (((0,), (0,)), ((), ())), preferred_element_type=F32)
    fsum[0:32, :] = total

    for c in range(nsteps):
        at = pl.ds(c * BLK, BLK)
        rows = node_ref[at, :]
        pre = (
            jnp.dot(rows, w1[0:512, :], preferred_element_type=F32)
            + jnp.dot(fsum[at, :].astype(BF), w1[512:1024, :], preferred_element_type=F32)
            + b1[...]
        )
        y = jnp.dot(silu(pre).astype(BF), w2[...], preferred_element_type=F32) + b2[...]
        new_nodes[at, :] = (rows.astype(F32) + norm_rows(y, gain[...], shift[...])).astype(BF)
        back.append(pltpu.make_async_copy(new_nodes.at[at], nodes_out.at[at], node_sem.at[c]))
        back[-1].start()
    for c in back:
        c.wait()


def node_call(rcv, edges, msg, coarse, inbound, nodes, w1, b1, w2, b2, gain, shift):
    E, N = msg.shape[0], nodes.shape[0]
    row = lambda v: v.reshape(1, -1)
    vm = pl.BlockSpec(memory_space=pltpu.VMEM)
    sm = pl.BlockSpec(memory_space=pltpu.SMEM)
    hbm = pl.BlockSpec(memory_space=pl.ANY)
    like = lambda v: pltpu.VMEM(v.shape, v.dtype)
    inbound = inbound.reshape(2048, 128)
    return pl.pallas_call(
        node_kernel,
        out_shape=tuple(jax.ShapeDtypeStruct(v.shape, BF) for v in (edges, coarse, nodes)),
        in_specs=[sm, vm] + [hbm] * 7 + [vm] * 4,
        out_specs=(hbm, hbm, hbm),
        scratch_shapes=[like(v) for v in (edges, msg, coarse, inbound, nodes, w1, w2, nodes)] + [
            pltpu.VMEM((N + WIN, D), F32), pltpu.VMEM((2048, 128), F32),
            pltpu.SemaphoreType.DMA((8,)), pltpu.SemaphoreType.DMA((8,)), pltpu.SemaphoreType.DMA((9,)),
            pltpu.SemaphoreType.DMA((5,)), pltpu.SemaphoreType.DMA((5,)),
        ],
        compiler_params=pltpu.CompilerParams(vmem_limit_bytes=60 * 2**20),
        cost_estimate=pl.CostEstimate(flops=3 * 10**9, bytes_accessed=16 * 10**6, transcendentals=10**6),
        name="nodes",
    )(rcv, row(rcv), edges, msg, coarse, inbound, nodes, w1, w2, row(b1), row(b2), row(gain), row(shift))


AXES = ("gx", "gy")


def on_device(
    node_feats, edge_feats, senders, receivers, send_lists, coarse_edges, coarse_senders, coarse_receivers,
    edge_w1, edge_b1, edge_w2, edge_b2, edge_gain, edge_shift,
    node_w1, node_b1, node_w2, node_b2, node_gain, node_shift,
):
    new_edges, message, new_coarse, inbound = edge_call(
        senders, receivers, coarse_senders, coarse_receivers, node_feats, send_lists, edge_feats, coarse_edges,
        edge_w1, edge_b1, edge_w2, edge_b2, edge_gain, edge_shift)
    new_edges, new_coarse, new_nodes = node_call(
        receivers, new_edges, message, new_coarse, inbound, node_feats,
        node_w1, node_b1, node_w2, node_b2, node_gain, node_shift)
    return new_nodes, new_edges, new_coarse


def solution(mesh):
    rows, flat, rep = P(AXES, None), P(AXES), P()
    return jax.shard_map(
        on_device, mesh=mesh,
        in_specs=(rows, rows, flat, flat, flat, rows, flat, flat) + (rep,) * 12,
        out_specs=(rows, rows, rows), check_vma=False,
    )
```

```python
import functools
import jax
import jax.numpy as jnp
from jax import lax
from jax.experimental import pallas as pl
from jax.experimental.pallas import tpu as pltpu
from jax.sharding import PartitionSpec as P

BF, F32 = jnp.bfloat16, jnp.float32
MESH = pl.DeviceIdType.MESH
D = 512
NCD = 20
BLK = 256
WIN = 264
PIECES = ((0, 32), (32, 32), (64, 16))
ORDERS = ((3, 2, 1), (2, 1, 3), (1, 3, 2))
SEGMENTS = ((0, 1), (1, 3), (3, 4), (4, 4), (4, 5), (5, 8))


def norm_rows(x, gain, shift):
    mean = jnp.mean(x, -1, keepdims=True)
    c = x - mean
    var = jnp.mean(c * c, -1, keepdims=True)
    return c * lax.rsqrt(var + 1e-05) * gain + shift


def silu(x):
    t = 0.5 * x
    return t + t * jnp.tanh(t)


def iota(shape, dim):
    return lax.broadcasted_iota(jnp.int32, shape, dim)


def coords(a, b):
    return lax.rem(a, 2), (a // 2) * 2 + b // 16, lax.rem(b // 4, 4), lax.rem(b, 4)


def device_at(core, z, x, y):
    return ((z // 2) * 2 + core, lax.rem(z, 2) * 16 + x * 4 + y)


def edge_kernel(
    snd, rcv, csnd, crcv,
    nodes_in, lists, edges_in, cedges, crow, w1_in, b1, w2_in, b2, gain, shift,
    edges_out, msg_out, new_coarse, inbound,
    node_ref, w1, w2, edges, new_edges, msg, p_snd, p_rcv, g_a, g_b,
    buf0, buf1, buf2, table, rows_s, rows_r, wide, outb, bound, halo, head32,
    send_sem, recv_sem, hsend_sem, hrecv_sem, out_send, in_recv, load_sem, store_sem,
):
    a, b = lax.axis_index("gx"), lax.axis_index("gy")
    me = coords(a, b)
    core = me[0]
    bufs = (buf0, buf1, buf2)
    nodes = node_ref.shape[0]

    loads = [
        pltpu.make_async_copy(src, dst, load_sem.at[k])
        for k, (src, dst) in enumerate(((nodes_in, node_ref), (w1_in, w1), (w2_in, w2), (edges_in, edges)))
    ]
    for c in loads:
        c.start()

    def peer(axis, step):
        c = list(me)
        c[axis] = lax.rem(c[axis] + step, 4)
        return device_at(*c)

    sibling = (a + 1 - 2 * core, b)
    halo_to = (
        (lax.rem(a + 1, 4), b), (lax.rem(a + 3, 4), b),
        (a, lax.rem(b + 1, 32)), (a, lax.rem(b + 31, 32)),
    )
    partners = [peer(axis, s) for axis in (1, 2, 3) for s in (1, 2, 3)] + [sibling] + list(halo_to)
    barrier = pltpu.get_barrier_semaphore()
    for p in partners:
        pl.semaphore_signal(barrier, inc=1, device_id=p, device_id_type=MESH)

    loads[0].wait()
    own = node_ref[0:32, :].astype(F32)
    for j in range(4):
        head32[pl.ds(j, 32, stride=4), :] = own[:, 128 * j:128 * (j + 1)]

    def slot(p):
        o = ORDERS[p]
        return ((core * 4 + me[o[2]]) * 4 + me[o[1]]) * 4 + me[o[0]]

    for p, (r0, n) in enumerate(PIECES):
        bufs[p][slot(p)] = head32[r0:r0 + n, :].astype(BF)

    hot = (iota((nodes, 128), 0) == lists[...]).astype(F32).astype(BF)
    bound[...] = lax.dot_general(
        hot, node_ref[...], (((0,), (0,)), ((), ())), preferred_element_type=F32).astype(BF)

    def block(p, step):
        return (core * 4 + lax.rem(me[ORDERS[p][2]] + 4 - step, 4)) * 16

    def send(p, first, size, to, k):
        part = bufs[p].at[pl.ds(first, size)]
        return pltpu.make_async_remote_copy(
            src_ref=part, dst_ref=part, send_sem=send_sem.at[p, k], recv_sem=recv_sem.at[p, k],
            device_id=to, device_id_type=MESH)

    started = []

    def go(copy):
        copy.start()
        started.append(copy)
        return copy

    def spread(p, stage):
        size = 4 ** stage
        first = slot(p) // size * size
        return [go(send(p, first, size, peer(ORDERS[p][stage], s), 3 * stage + s - 1)) for s in (2, 1, 3)]

    def across(p, first, size, k):
        return go(send(p, first, size, sibling, k))

    def arrived(copies):
        for c in copies:
            c.wait_recv()

    def project(rows, lo, tab, at, bias):
        n = rows.shape[0]
        v = jnp.dot(rows, w1[lo:lo + 512, :], preferred_element_type=F32)
        if bias is not None:
            v = v + bias
        for j in range(4):
            tab[pl.ds(at, n), j, :] = v[:, 128 * j:128 * (j + 1)]

    def project_own(lo, hi):
        @pl.loop(lo, hi)
        def _(c):
            at = pl.multiple_of(c * 256, 256)
            rows = node_ref[pl.ds(at, 256), :]
            project(rows, 512, p_snd, at, None)
            project(rows, 1024, p_rcv, at, b1[...])

    def gather(k, g, lo=0, hi=BLK):
        base = k * BLK
        for e in range(lo, hi):
            g[pl.ds(4 * e, 4), :] = p_snd[snd[base + e]] + p_rcv[rcv[base + e]]

    def first(k, g):
        x = edges[pl.ds(pl.multiple_of(k * BLK, BLK), BLK), :]
        pre = jnp.dot(x, w1[0:512, :], preferred_element_type=F32)
        pre = pre + jnp.concatenate([g[pl.ds(j, BLK, stride=4), :] for j in range(4)], 1)
        return silu(pre).astype(BF)

    def second(h):
        return jnp.dot(h, w2[...], preferred_element_type=F32) + b2[...]

    def third(k, y):
        at = pl.multiple_of(k * BLK, BLK)
        m = norm_rows(y, gain[...], shift[...])
        new_edges[pl.ds(at, BLK), :] = (edges[pl.ds(at, BLK), :].astype(F32) + m).astype(BF)
        msg[pl.ds(at, BLK), :] = m.astype(BF)

    last = edges.shape[0] // BLK - 1

    def stores(i):
        part = pl.ds(pl.multiple_of(i * 2 * BLK, 2 * BLK), 2 * BLK)
        return (
            pltpu.make_async_copy(new_edges.at[part], edges_out.at[part], store_sem.at[0, i]),
            pltpu.make_async_copy(msg.at[part], msg_out.at[part], store_sem.at[1, i]),
        )

    def pairs(lo, hi):
        @pl.loop(lo, hi)
        def _(i):
            half = BLK // 2
            k, n = 2 * i, jnp.minimum(2 * i + 2, last - 1)
            h_a = first(k, g_a)
            h_b = first(k + 1, g_b)
            gather(n, g_a, 0, half)
            y_a = second(h_a)
            gather(n, g_a, half, BLK)
            y_b = second(h_b)
            gather(n + 1, g_b, 0, half)
            third(k, y_a)
            gather(n + 1, g_b, half, BLK)
            third(k + 1, y_b)
            for c in stores(i):
                c.start()

    def fill(c):
        @pl.loop(0, 64)
        def _(q):
            u, v, w = q // 16, lax.rem(q // 4, 4), lax.rem(q, 4)
            for p, (r0, n) in enumerate(PIECES):
                pos = {ORDERS[p][2]: u, ORDERS[p][1]: v, ORDERS[p][0]: w}
                aa, bb = device_at(c, pos[1], pos[2], pos[3])
                table[pl.ds((aa * 32 + bb) * NCD + r0 // 4, n // 4)] = (
                    bufs[p][c * 64 + q].astype(F32).reshape(n // 4, 4, 128))

    pl.semaphore_wait(barrier, len(partners))
    one = [spread(p, 0) for p in range(3)]
    halos = []
    for k, to in enumerate(halo_to):
        halos.append(go(pltpu.make_async_remote_copy(
            src_ref=bound, dst_ref=halo.at[pl.ds(128 * k, 128)], send_sem=hsend_sem.at[k], recv_sem=hrecv_sem.at[k],
            device_id=to, device_id_type=MESH)))
    loads[1].wait()
    project_own(0, nodes // 256)
    two = []
    for p in range(3):
        arrived(one[p])
        two.append(spread(p, 1))
    for k in range(4):
        halos[k].wait_recv()
    for k in range(2):
        project(halo[256 * k:256 * (k + 1), :], 512, p_snd, nodes + 256 * k, None)
    loads[2].wait()
    loads[3].wait()
    gather(0, g_a)
    gather(1, g_b)
    pairs(*SEGMENTS[0])
    three, cross = [], []
    for p in range(3):
        arrived(two[p])
        three.append(spread(p, 2))
    for p in range(3):
        cross.append(across(p, block(p, 0), 16, 10))
    pairs(*SEGMENTS[1])
    for i, s in enumerate((2, 1, 3)):
        for p in range(3):
            three[p][i].wait_recv()
            cross.append(across(p, block(p, s), 16, 10 + s))
        if i < 2:
            pairs(*SEGMENTS[2 + i])
    fill(core)
    pairs(*SEGMENTS[4])
    arrived(cross)
    fill(1 - core)

    ce = cedges.shape[0]
    for e in range(ce):
        rows_s[pl.ds(4 * e, 4), :] = table[csnd[e]]
        rows_r[pl.ds(4 * e, 4), :] = table[crcv[e]]
    x = cedges[...]
    take = lambda ref: jnp.concatenate([ref[pl.ds(j, ce, stride=4), :] for j in range(4)], 1).astype(BF)
    pre = (
        jnp.dot(x, w1[0:512, :], preferred_element_type=F32)
        + jnp.dot(take(rows_s), w1[512:1024, :], preferred_element_type=F32)
        + jnp.dot(take(rows_r), w1[1024:1536, :], preferred_element_type=F32)
        + b1[...]
    )
    y = jnp.dot(silu(pre).astype(BF), w2[...], preferred_element_type=F32) + b2[...]
    m = norm_rows(y, gain[...], shift[...])
    new_coarse[...] = (x.astype(F32) + m).astype(BF)
    mb = m.astype(BF)

    c = crow[...]
    owner = lax.shift_right_logical(c * 52429, 20)
    local = c - owner * NCD
    own_hot = (iota((128, ce), 0) == owner).astype(F32)
    before = (iota((ce, ce), 0) < iota((ce, ce), 1)).astype(F32).astype(BF)
    counts = jnp.dot(own_hot.astype(BF), before, preferred_element_type=F32)
    rank = jnp.sum(own_hot * counts, axis=0, keepdims=True)
    for s in range(3):
        placed = jnp.where(rank == s, own_hot, 0.0).astype(BF)
        got = jnp.dot(placed, mb, preferred_element_type=F32)
        for j in range(4):
            wide[pl.ds(4 * s + j, 128, stride=16), :] = got[:, 128 * j:128 * (j + 1)]
    tags = (iota((128, ce), 0).astype(F32) == rank * 32.0 + local.astype(F32)).astype(F32).astype(BF)
    wide[pl.ds(12, 128, stride=16), :] = lax.dot_general(
        own_hot.astype(BF), tags, (((1,), (1,)), ((), ())), preferred_element_type=F32)
    for j in range(1, 4):
        wide[pl.ds(12 + j, 128, stride=16), :] = jnp.zeros((128, 128), F32)
    outb[...] = wide[...].astype(BF).reshape(128, 16, 128)

    g = a * 32 + b
    inbound[0] = outb[g]

    @pl.loop(1, 128)
    def _(k):
        to = lax.rem(g + k, 128)
        pltpu.make_async_remote_copy(
            src_ref=outb.at[to], dst_ref=inbound.at[k], send_sem=out_send, recv_sem=in_recv,
            device_id=(to // 32, lax.rem(to, 32)), device_id_type=MESH).start()

    pairs(*SEGMENTS[5])

    most = pl.ds(1, 127)
    pltpu.make_async_copy(inbound.at[most], inbound.at[most], in_recv).wait()
    pltpu.make_async_copy(outb.at[most], outb.at[most], out_send).wait()
    for k in started:
        k.wait_send()
    for i in range(edges.shape[0] // (2 * BLK)):
        for c in stores(i):
            c.wait()


def edge_call(snd, rcv, csnd, crcv, nodes, lists, edges, cedges, w1, b1, w2, b2, gain, shift):
    row = lambda v: v.reshape(1, -1)
    vm = pl.BlockSpec(memory_space=pltpu.VMEM)
    sm = pl.BlockSpec(memory_space=pltpu.SMEM)
    hbm = pl.BlockSpec(memory_space=pl.ANY)
    ce, E, N = cedges.shape[0], edges.shape[0], nodes.shape[0]
    return pl.pallas_call(
        edge_kernel,
        out_shape=(
            jax.ShapeDtypeStruct((E, D), BF),
            jax.ShapeDtypeStruct((E, D), BF),
            jax.ShapeDtypeStruct((ce, D), BF),
            jax.ShapeDtypeStruct((128, 16, 128), BF),
        ),
        in_specs=[sm] * 4 + [hbm, vm, hbm, vm, vm, hbm, vm, hbm] + [vm] * 3,
        out_specs=(hbm, hbm, vm, vm),
        scratch_shapes=[
            pltpu.VMEM((N, D), BF), pltpu.VMEM((3 * D, D), BF), pltpu.VMEM((D, D), BF),
            pltpu.VMEM((E, D), BF), pltpu.VMEM((E, D), BF), pltpu.VMEM((E, D), BF),
            pltpu.VMEM((N + 512, 4, 128), F32), pltpu.VMEM((N, 4, 128), F32),
            pltpu.VMEM((BLK * 4, 128), F32), pltpu.VMEM((BLK * 4, 128), F32),
            pltpu.VMEM((128, 32, 128), BF), pltpu.VMEM((128, 32, 128), BF), pltpu.VMEM((128, 16, 128), BF),
            pltpu.VMEM((128 * NCD, 4, 128), F32),
            pltpu.VMEM((ce * 4, 128), F32), pltpu.VMEM((ce * 4, 128), F32),
            pltpu.VMEM((2048, 128), F32), pltpu.VMEM((128, 16, 128), BF),
            pltpu.VMEM((128, D), BF), pltpu.VMEM((512, D), BF), pltpu.VMEM((128, 128), F32),
            pltpu.SemaphoreType.DMA((3, 14)), pltpu.SemaphoreType.DMA((3, 14)),
            pltpu.SemaphoreType.DMA((4,)), pltpu.SemaphoreType.DMA((4,)),
            pltpu.SemaphoreType.DMA, pltpu.SemaphoreType.DMA,
            pltpu.SemaphoreType.DMA((4,)), pltpu.SemaphoreType.DMA((2, 8)),
        ],
        compiler_params=pltpu.CompilerParams(
            collective_id=0, has_side_effects=True, vmem_limit_bytes=60 * 2**20),
        cost_estimate=pl.CostEstimate(flops=7 * 10**9, bytes_accessed=2 * 10**7, transcendentals=2 * 10**6),
        name="edges",
    )(snd, rcv, csnd, crcv, nodes, row(lists), edges, cedges, row(crcv), w1, row(b1), w2, row(b2), row(gain), row(shift))


def node_kernel(
    rcv,
    rrow, edges_in, msg_in, coarse_in, inbound_in, nodes_in, w1_in, w2_in, b1, b2, gain, shift,
    edges_out, coarse_out, nodes_out,
    edges, msg, coarse, inbound, node_ref, w1, w2, new_nodes, fsum, wide,
    msg_sem, edge_sem, back_sem, small_sem, node_sem,
):
    steps, nsteps = msg.shape[0] // (2 * BLK), node_ref.shape[0] // BLK
    part = lambda i: pl.ds(2 * BLK * i, 2 * BLK)
    loads = [pltpu.make_async_copy(msg_in.at[part(i)], msg.at[part(i)], msg_sem.at[i]) for i in range(steps)]
    small = [
        pltpu.make_async_copy(src, dst, small_sem.at[k]) for k, (src, dst) in enumerate((
            (nodes_in, node_ref), (w1_in, w1), (w2_in, w2), (inbound_in, inbound), (coarse_in, coarse)))
    ]
    there = [pltpu.make_async_copy(edges_in.at[part(i)], edges.at[part(i)], edge_sem.at[i]) for i in range(steps)]
    back = [pltpu.make_async_copy(edges.at[part(i)], edges_out.at[part(i)], back_sem.at[i]) for i in range(steps)]
    back.append(pltpu.make_async_copy(coarse, coarse_out, back_sem.at[steps]))
    for c in loads + small + there:
        c.start()
    fsum[...] = jnp.zeros_like(fsum)
    for i in range(steps):
        loads[i].wait()
        for k in (2 * i, 2 * i + 1):
            start = pl.multiple_of((rcv[k * BLK] // 8) * 8, 8)
            ids = rrow[:, k * BLK:(k + 1) * BLK]
            hot = (ids - start == iota((WIN, BLK), 0)).astype(F32).astype(BF)
            fsum[pl.ds(start, WIN), :] += jnp.dot(hot, msg[k * BLK:(k + 1) * BLK, :], preferred_element_type=F32)
    for c in small:
        c.wait()
    back[steps].start()
    for i in range(steps):
        there[i].wait()
        back[i].start()

    wide[...] = inbound[...].astype(F32)
    tags = wide[pl.ds(12, 128, stride=16), :].astype(BF)
    total = fsum[0:32, :]
    for s in range(3):
        got = jnp.concatenate([wide[pl.ds(4 * s + j, 128, stride=16), :] for j in range(4)], 1).astype(BF)
        total = total + lax.dot_general(
            tags[:, 32 * s:32 * s + 32], got, (((0,), (0,)), ((), ())), preferred_element_type=F32)
    fsum[0:32, :] = total

    for c in range(nsteps):
        at = pl.ds(c * BLK, BLK)
        rows = node_ref[at, :]
        pre = (
            jnp.dot(rows, w1[0:512, :], preferred_element_type=F32)
            + jnp.dot(fsum[at, :].astype(BF), w1[512:1024, :], preferred_element_type=F32)
            + b1[...]
        )
        y = jnp.dot(silu(pre).astype(BF), w2[...], preferred_element_type=F32) + b2[...]
        new_nodes[at, :] = (rows.astype(F32) + norm_rows(y, gain[...], shift[...])).astype(BF)
        back.append(pltpu.make_async_copy(new_nodes.at[at], nodes_out.at[at], node_sem.at[c]))
        back[-1].start()
    for c in back:
        c.wait()


def node_call(rcv, edges, msg, coarse, inbound, nodes, w1, b1, w2, b2, gain, shift):
    E, N = msg.shape[0], nodes.shape[0]
    row = lambda v: v.reshape(1, -1)
    vm = pl.BlockSpec(memory_space=pltpu.VMEM)
    sm = pl.BlockSpec(memory_space=pltpu.SMEM)
    hbm = pl.BlockSpec(memory_space=pl.ANY)
    like = lambda v: pltpu.VMEM(v.shape, v.dtype)
    inbound = inbound.reshape(2048, 128)
    return pl.pallas_call(
        node_kernel,
        out_shape=tuple(jax.ShapeDtypeStruct(v.shape, BF) for v in (edges, coarse, nodes)),
        in_specs=[sm, vm] + [hbm] * 7 + [vm] * 4,
        out_specs=(hbm, hbm, hbm),
        scratch_shapes=[like(v) for v in (edges, msg, coarse, inbound, nodes, w1, w2, nodes)] + [
            pltpu.VMEM((N + WIN, D), F32), pltpu.VMEM((2048, 128), F32),
            pltpu.SemaphoreType.DMA((8,)), pltpu.SemaphoreType.DMA((8,)), pltpu.SemaphoreType.DMA((9,)),
            pltpu.SemaphoreType.DMA((5,)), pltpu.SemaphoreType.DMA((5,)),
        ],
        compiler_params=pltpu.CompilerParams(vmem_limit_bytes=60 * 2**20),
        cost_estimate=pl.CostEstimate(flops=3 * 10**9, bytes_accessed=16 * 10**6, transcendentals=10**6),
        name="nodes",
    )(rcv, row(rcv), edges, msg, coarse, inbound, nodes, w1, w2, row(b1), row(b2), row(gain), row(shift))


AXES = ("gx", "gy")


def on_device(
    node_feats, edge_feats, senders, receivers, send_lists, coarse_edges, coarse_senders, coarse_receivers,
    edge_w1, edge_b1, edge_w2, edge_b2, edge_gain, edge_shift,
    node_w1, node_b1, node_w2, node_b2, node_gain, node_shift,
):
    new_edges, message, new_coarse, inbound = edge_call(
        senders, receivers, coarse_senders, coarse_receivers, node_feats, send_lists, edge_feats, coarse_edges,
        edge_w1, edge_b1, edge_w2, edge_b2, edge_gain, edge_shift)
    new_edges, new_coarse, new_nodes = node_call(
        receivers, new_edges, message, new_coarse, inbound, node_feats,
        node_w1, node_b1, node_w2, node_b2, node_gain, node_shift)
    return new_nodes, new_edges, new_coarse


def solution(mesh):
    rows, flat, rep = P(AXES, None), P(AXES), P()
    return jax.shard_map(
        on_device, mesh=mesh,
        in_specs=(rows, rows, flat, flat, flat, rows, flat, flat) + (rep,) * 12,
        out_specs=(rows, rows, rows), check_vma=False,
    )
```

```python
import functools
import jax
import jax.numpy as jnp
from jax import lax
from jax.experimental import pallas as pl
from jax.experimental.pallas import tpu as pltpu
from jax.sharding import PartitionSpec as P

BF, F32 = jnp.bfloat16, jnp.float32
MESH = pl.DeviceIdType.MESH
D = 512
NCD = 20
BLK = 256
WIN = 264
PIECES = ((0, 32), (32, 32), (64, 16))
ORDERS = ((3, 2, 1), (2, 1, 3), (1, 3, 2))
SEGMENTS = ((0, 1), (1, 3), (3, 4), (4, 4), (4, 5), (5, 8))


def norm_rows(x, gain, shift):
    mean = jnp.mean(x, -1, keepdims=True)
    c = x - mean
    var = jnp.mean(c * c, -1, keepdims=True)
    return c * lax.rsqrt(var + 1e-05) * gain + shift


def silu(x):
    t = 0.5 * x
    return t + t * jnp.tanh(t)


def iota(shape, dim):
    return lax.broadcasted_iota(jnp.int32, shape, dim)


def coords(a, b):
    return lax.rem(a, 2), (a // 2) * 2 + b // 16, lax.rem(b // 4, 4), lax.rem(b, 4)


def device_at(core, z, x, y):
    return ((z // 2) * 2 + core, lax.rem(z, 2) * 16 + x * 4 + y)


def edge_kernel(
    snd, rcv, csnd, crcv,
    nodes_in, lists, edges_in, cedges, crow, w1_in, b1, w2_in, b2, gain, shift,
    new_edges, msg, new_coarse, inbound,
    node_ref, w1, w2, edges, p_snd, p_rcv, g_a, g_b,
    buf0, buf1, buf2, table, rows_s, rows_r, wide, outb, bound, halo, head32,
    send_sem, recv_sem, hsend_sem, hrecv_sem, out_send, in_recv, load_sem,
):
    a, b = lax.axis_index("gx"), lax.axis_index("gy")
    me = coords(a, b)
    core = me[0]
    bufs = (buf0, buf1, buf2)
    nodes = node_ref.shape[0]

    loads = [
        pltpu.make_async_copy(src, dst, load_sem.at[k])
        for k, (src, dst) in enumerate(((nodes_in, node_ref), (w1_in, w1), (w2_in, w2), (edges_in, edges)))
    ]
    for c in loads:
        c.start()

    def peer(axis, step):
        c = list(me)
        c[axis] = lax.rem(c[axis] + step, 4)
        return device_at(*c)

    sibling = (a + 1 - 2 * core, b)
    halo_to = (
        (lax.rem(a + 1, 4), b), (lax.rem(a + 3, 4), b),
        (a, lax.rem(b + 1, 32)), (a, lax.rem(b + 31, 32)),
    )
    partners = [peer(axis, s) for axis in (1, 2, 3) for s in (1, 2, 3)] + [sibling] + list(halo_to)
    barrier = pltpu.get_barrier_semaphore()
    for p in partners:
        pl.semaphore_signal(barrier, inc=1, device_id=p, device_id_type=MESH)

    loads[0].wait()
    own = node_ref[0:32, :].astype(F32)
    for j in range(4):
        head32[pl.ds(j, 32, stride=4), :] = own[:, 128 * j:128 * (j + 1)]

    def slot(p):
        o = ORDERS[p]
        return ((core * 4 + me[o[2]]) * 4 + me[o[1]]) * 4 + me[o[0]]

    for p, (r0, n) in enumerate(PIECES):
        bufs[p][slot(p)] = head32[r0:r0 + n, :].astype(BF)

    hot = (iota((nodes, 128), 0) == lists[...]).astype(F32).astype(BF)
    bound[...] = lax.dot_general(
        hot, node_ref[...], (((0,), (0,)), ((), ())), preferred_element_type=F32).astype(BF)

    def block(p, step):
        return (core * 4 + lax.rem(me[ORDERS[p][2]] + 4 - step, 4)) * 16

    def send(p, first, size, to, k):
        part = bufs[p].at[pl.ds(first, size)]
        return pltpu.make_async_remote_copy(
            src_ref=part, dst_ref=part, send_sem=send_sem.at[p, k], recv_sem=recv_sem.at[p, k],
            device_id=to, device_id_type=MESH)

    started = []

    def go(copy):
        copy.start()
        started.append(copy)
        return copy

    def spread(p, stage):
        size = 4 ** stage
        first = slot(p) // size * size
        return [go(send(p, first, size, peer(ORDERS[p][stage], s), 3 * stage + s - 1)) for s in (2, 1, 3)]

    def across(p, first, size, k):
        return go(send(p, first, size, sibling, k))

    def arrived(copies):
        for c in copies:
            c.wait_recv()

    def project(rows, lo, tab, at, bias):
        n = rows.shape[0]
        v = jnp.dot(rows, w1[lo:lo + 512, :], preferred_element_type=F32)
        if bias is not None:
            v = v + bias
        for j in range(4):
            tab[pl.ds(at, n), j, :] = v[:, 128 * j:128 * (j + 1)]

    def project_own(lo, hi):
        @pl.loop(lo, hi)
        def _(c):
            at = pl.multiple_of(c * 256, 256)
            rows = node_ref[pl.ds(at, 256), :]
            project(rows, 512, p_snd, at, None)
            project(rows, 1024, p_rcv, at, b1[...])

    def gather(k, g, lo=0, hi=BLK):
        base = k * BLK
        for e in range(lo, hi):
            g[pl.ds(4 * e, 4), :] = p_snd[snd[base + e]] + p_rcv[rcv[base + e]]

    def first(k, g):
        x = edges[pl.ds(pl.multiple_of(k * BLK, BLK), BLK), :]
        pre = jnp.dot(x, w1[0:512, :], preferred_element_type=F32)
        pre = pre + jnp.concatenate([g[pl.ds(j, BLK, stride=4), :] for j in range(4)], 1)
        return silu(pre).astype(BF)

    def second(h):
        return jnp.dot(h, w2[...], preferred_element_type=F32) + b2[...]

    def third(k, y):
        at = pl.multiple_of(k * BLK, BLK)
        m = norm_rows(y, gain[...], shift[...])
        new_edges[pl.ds(at, BLK), :] = (edges[pl.ds(at, BLK), :].astype(F32) + m).astype(BF)
        msg[pl.ds(at, BLK), :] = m.astype(BF)

    last = edges.shape[0] // BLK - 1

    def pairs(lo, hi):
        @pl.loop(lo, hi)
        def _(i):
            half = BLK // 2
            k, n = 2 * i, jnp.minimum(2 * i + 2, last - 1)
            h_a = first(k, g_a)
            h_b = first(k + 1, g_b)
            gather(n, g_a, 0, half)
            y_a = second(h_a)
            gather(n, g_a, half, BLK)
            y_b = second(h_b)
            gather(n + 1, g_b, 0, half)
            third(k, y_a)
            gather(n + 1, g_b, half, BLK)
            third(k + 1, y_b)

    def fill(c):
        @pl.loop(0, 64)
        def _(q):
            u, v, w = q // 16, lax.rem(q // 4, 4), lax.rem(q, 4)
            for p, (r0, n) in enumerate(PIECES):
                pos = {ORDERS[p][2]: u, ORDERS[p][1]: v, ORDERS[p][0]: w}
                aa, bb = device_at(c, pos[1], pos[2], pos[3])
                table[pl.ds((aa * 32 + bb) * NCD + r0 // 4, n // 4)] = (
                    bufs[p][c * 64 + q].astype(F32).reshape(n // 4, 4, 128))

    pl.semaphore_wait(barrier, len(partners))
    one = [spread(p, 0) for p in range(3)]
    halos = []
    for k, to in enumerate(halo_to):
        halos.append(go(pltpu.make_async_remote_copy(
            src_ref=bound, dst_ref=halo.at[pl.ds(128 * k, 128)], send_sem=hsend_sem.at[k], recv_sem=hrecv_sem.at[k],
            device_id=to, device_id_type=MESH)))
    loads[1].wait()
    project_own(0, nodes // 256)
    two = []
    for p in range(3):
        arrived(one[p])
        two.append(spread(p, 1))
    for k in range(4):
        halos[k].wait_recv()
    for k in range(2):
        project(halo[256 * k:256 * (k + 1), :], 512, p_snd, nodes + 256 * k, None)
    loads[2].wait()
    loads[3].wait()
    gather(0, g_a)
    gather(1, g_b)
    pairs(*SEGMENTS[0])
    three, cross = [], []
    for p in range(3):
        arrived(two[p])
        three.append(spread(p, 2))
    for p in range(3):
        cross.append(across(p, block(p, 0), 16, 10))
    pairs(*SEGMENTS[1])
    for i, s in enumerate((2, 1, 3)):
        for p in range(3):
            three[p][i].wait_recv()
            cross.append(across(p, block(p, s), 16, 10 + s))
        if i < 2:
            pairs(*SEGMENTS[2 + i])
    fill(core)
    pairs(*SEGMENTS[4])
    arrived(cross)
    fill(1 - core)

    ce = cedges.shape[0]
    for e in range(ce):
        rows_s[pl.ds(4 * e, 4), :] = table[csnd[e]]
        rows_r[pl.ds(4 * e, 4), :] = table[crcv[e]]
    x = cedges[...]
    take = lambda ref: jnp.concatenate([ref[pl.ds(j, ce, stride=4), :] for j in range(4)], 1).astype(BF)
    pre = (
        jnp.dot(x, w1[0:512, :], preferred_element_type=F32)
        + jnp.dot(take(rows_s), w1[512:1024, :], preferred_element_type=F32)
        + jnp.dot(take(rows_r), w1[1024:1536, :], preferred_element_type=F32)
        + b1[...]
    )
    y = jnp.dot(silu(pre).astype(BF), w2[...], preferred_element_type=F32) + b2[...]
    m = norm_rows(y, gain[...], shift[...])
    new_coarse[...] = (x.astype(F32) + m).astype(BF)
    mb = m.astype(BF)

    c = crow[...]
    owner = lax.shift_right_logical(c * 52429, 20)
    local = c - owner * NCD
    own_hot = (iota((128, ce), 0) == owner).astype(F32)
    before = (iota((ce, ce), 0) < iota((ce, ce), 1)).astype(F32).astype(BF)
    counts = jnp.dot(own_hot.astype(BF), before, preferred_element_type=F32)
    rank = jnp.sum(own_hot * counts, axis=0, keepdims=True)
    for s in range(3):
        placed = jnp.where(rank == s, own_hot, 0.0).astype(BF)
        got = jnp.dot(placed, mb, preferred_element_type=F32)
        for j in range(4):
            wide[pl.ds(4 * s + j, 128, stride=16), :] = got[:, 128 * j:128 * (j + 1)]
    tags = (iota((128, ce), 0).astype(F32) == rank * 32.0 + local.astype(F32)).astype(F32).astype(BF)
    wide[pl.ds(12, 128, stride=16), :] = lax.dot_general(
        own_hot.astype(BF), tags, (((1,), (1,)), ((), ())), preferred_element_type=F32)
    for j in range(1, 4):
        wide[pl.ds(12 + j, 128, stride=16), :] = jnp.zeros((128, 128), F32)
    outb[...] = wide[...].astype(BF).reshape(128, 16, 128)

    g = a * 32 + b
    inbound[0] = outb[g]

    @pl.loop(1, 128)
    def _(k):
        to = lax.rem(g + k, 128)
        pltpu.make_async_remote_copy(
            src_ref=outb.at[to], dst_ref=inbound.at[k], send_sem=out_send, recv_sem=in_recv,
            device_id=(to // 32, lax.rem(to, 32)), device_id_type=MESH).start()

    pairs(*SEGMENTS[5])

    most = pl.ds(1, 127)
    pltpu.make_async_copy(inbound.at[most], inbound.at[most], in_recv).wait()
    pltpu.make_async_copy(outb.at[most], outb.at[most], out_send).wait()
    for k in started:
        k.wait_send()


def edge_call(snd, rcv, csnd, crcv, nodes, lists, edges, cedges, w1, b1, w2, b2, gain, shift):
    row = lambda v: v.reshape(1, -1)
    vm = pl.BlockSpec(memory_space=pltpu.VMEM)
    sm = pl.BlockSpec(memory_space=pltpu.SMEM)
    hbm = pl.BlockSpec(memory_space=pl.ANY)
    ce, E, N = cedges.shape[0], edges.shape[0], nodes.shape[0]
    return pl.pallas_call(
        edge_kernel,
        out_shape=(
            pltpu.VMEM((E, D), BF),
            pltpu.VMEM((E, D), BF),
            jax.ShapeDtypeStruct((ce, D), BF),
            jax.ShapeDtypeStruct((128, 16, 128), BF),
        ),
        in_specs=[sm] * 4 + [hbm, vm, hbm, vm, vm, hbm, vm, hbm] + [vm] * 3,
        out_specs=(vm, vm, vm, vm),
        scratch_shapes=[
            pltpu.VMEM((N, D), BF), pltpu.VMEM((3 * D, D), BF), pltpu.VMEM((D, D), BF),
            pltpu.VMEM((E, D), BF),
            pltpu.VMEM((N + 512, 4, 128), F32), pltpu.VMEM((N, 4, 128), F32),
            pltpu.VMEM((BLK * 4, 128), F32), pltpu.VMEM((BLK * 4, 128), F32),
            pltpu.VMEM((128, 32, 128), BF), pltpu.VMEM((128, 32, 128), BF), pltpu.VMEM((128, 16, 128), BF),
            pltpu.VMEM((128 * NCD, 4, 128), F32),
            pltpu.VMEM((ce * 4, 128), F32), pltpu.VMEM((ce * 4, 128), F32),
            pltpu.VMEM((2048, 128), F32), pltpu.VMEM((128, 16, 128), BF),
            pltpu.VMEM((128, D), BF), pltpu.VMEM((512, D), BF), pltpu.VMEM((128, 128), F32),
            pltpu.SemaphoreType.DMA((3, 14)), pltpu.SemaphoreType.DMA((3, 14)),
            pltpu.SemaphoreType.DMA((4,)), pltpu.SemaphoreType.DMA((4,)),
            pltpu.SemaphoreType.DMA, pltpu.SemaphoreType.DMA,
            pltpu.SemaphoreType.DMA((4,)),
        ],
        compiler_params=pltpu.CompilerParams(
            collective_id=0, has_side_effects=True, vmem_limit_bytes=54 * 2**20),
        cost_estimate=pl.CostEstimate(flops=7 * 10**9, bytes_accessed=2 * 10**7, transcendentals=2 * 10**6),
        name="edges",
    )(*(pltpu.with_memory_space_constraint(v, pltpu.HBM) for v in (
        snd, rcv, csnd, crcv, nodes, row(lists), edges, cedges, row(crcv), w1, row(b1), w2, row(b2), row(gain), row(shift))))


def node_kernel(
    rcv,
    rrow, edges, msg, coarse_in, inbound_in, nodes_in, w1_in, w2_in, b1, b2, gain, shift,
    edges_out, coarse_out, nodes_out,
    coarse, inbound, node_ref, w1, w2, new_nodes, fsum, wide,
    back_sem, small_sem, node_sem,
):
    steps, nsteps = msg.shape[0] // (2 * BLK), node_ref.shape[0] // BLK
    part = lambda i: pl.ds(2 * BLK * i, 2 * BLK)
    small = [
        pltpu.make_async_copy(src, dst, small_sem.at[k]) for k, (src, dst) in enumerate((
            (nodes_in, node_ref), (w1_in, w1), (w2_in, w2), (inbound_in, inbound), (coarse_in, coarse)))
    ]
    back = [pltpu.make_async_copy(edges.at[part(i)], edges_out.at[part(i)], back_sem.at[i]) for i in range(steps)]
    back.append(pltpu.make_async_copy(coarse, coarse_out, back_sem.at[steps]))
    for c in small + back[:steps]:
        c.start()
    fsum[...] = jnp.zeros_like(fsum)
    for i in range(steps):
        for k in (2 * i, 2 * i + 1):
            start = pl.multiple_of((rcv[k * BLK] // 8) * 8, 8)
            narrow = rcv[(k + 1) * BLK - 1] - start < 128

            def add(rows):
                ids = rrow[:, k * BLK:(k + 1) * BLK]
                hot = (ids - start == iota((rows, BLK), 0)).astype(F32).astype(BF)
                fsum[pl.ds(start, rows), :] += jnp.dot(
                    hot, msg[k * BLK:(k + 1) * BLK, :], preferred_element_type=F32)

            pl.when(narrow)(functools.partial(add, 128))
            pl.when(jnp.logical_not(narrow))(functools.partial(add, WIN))
    for c in small:
        c.wait()
    back[steps].start()
    wide[...] = inbound[...].astype(F32)
    tags = wide[pl.ds(12, 128, stride=16), :].astype(BF)
    total = fsum[0:32, :]
    for s in range(3):
        got = jnp.concatenate([wide[pl.ds(4 * s + j, 128, stride=16), :] for j in range(4)], 1).astype(BF)
        total = total + lax.dot_general(
            tags[:, 32 * s:32 * s + 32], got, (((0,), (0,)), ((), ())), preferred_element_type=F32)
    fsum[0:32, :] = total

    for c in range(nsteps):
        at = pl.ds(c * BLK, BLK)
        rows = node_ref[at, :]
        pre = (
            jnp.dot(rows, w1[0:512, :], preferred_element_type=F32)
            + jnp.dot(fsum[at, :].astype(BF), w1[512:1024, :], preferred_element_type=F32)
            + b1[...]
        )
        y = jnp.dot(silu(pre).astype(BF), w2[...], preferred_element_type=F32) + b2[...]
        new_nodes[at, :] = (rows.astype(F32) + norm_rows(y, gain[...], shift[...])).astype(BF)
        back.append(pltpu.make_async_copy(new_nodes.at[at], nodes_out.at[at], node_sem.at[c]))
        back[-1].start()
    for c in back:
        c.wait()


def node_call(rcv, edges, msg, coarse, inbound, nodes, w1, b1, w2, b2, gain, shift):
    E, N = msg.shape[0], nodes.shape[0]
    row = lambda v: v.reshape(1, -1)
    vm = pl.BlockSpec(memory_space=pltpu.VMEM)
    sm = pl.BlockSpec(memory_space=pltpu.SMEM)
    hbm = pl.BlockSpec(memory_space=pl.ANY)
    like = lambda v: pltpu.VMEM(v.shape, v.dtype)
    inbound = inbound.reshape(2048, 128)
    return pl.pallas_call(
        node_kernel,
        out_shape=tuple(jax.ShapeDtypeStruct(v.shape, BF) for v in (edges, coarse, nodes)),
        in_specs=[sm, vm, vm, vm] + [hbm] * 5 + [vm] * 4,
        out_specs=(hbm, hbm, hbm),
        scratch_shapes=[like(v) for v in (coarse, inbound, nodes, w1, w2, nodes)] + [
            pltpu.VMEM((N + WIN, D), F32), pltpu.VMEM((2048, 128), F32),
            pltpu.SemaphoreType.DMA((9,)),
            pltpu.SemaphoreType.DMA((5,)), pltpu.SemaphoreType.DMA((5,)),
        ],
        compiler_params=pltpu.CompilerParams(vmem_limit_bytes=40 * 2**20),
        cost_estimate=pl.CostEstimate(flops=3 * 10**9, bytes_accessed=16 * 10**6, transcendentals=10**6),
        name="nodes",
    )(*(pltpu.with_memory_space_constraint(v, pltpu.HBM) for v in (rcv, row(rcv))),
      *(pltpu.with_memory_space_constraint(v, pltpu.VMEM) for v in (edges, msg)),
      *(pltpu.with_memory_space_constraint(v, pltpu.HBM) for v in (
          coarse, inbound, nodes, w1, w2, row(b1), row(b2), row(gain), row(shift))))


AXES = ("gx", "gy")


def on_device(
    node_feats, edge_feats, senders, receivers, send_lists, coarse_edges, coarse_senders, coarse_receivers,
    edge_w1, edge_b1, edge_w2, edge_b2, edge_gain, edge_shift,
    node_w1, node_b1, node_w2, node_b2, node_gain, node_shift,
):
    new_edges, message, new_coarse, inbound = edge_call(
        senders, receivers, coarse_senders, coarse_receivers, node_feats, send_lists, edge_feats, coarse_edges,
        edge_w1, edge_b1, edge_w2, edge_b2, edge_gain, edge_shift)
    new_edges, new_coarse, new_nodes = node_call(
        receivers, new_edges, message, new_coarse, inbound, node_feats,
        node_w1, node_b1, node_w2, node_b2, node_gain, node_shift)
    return new_nodes, new_edges, new_coarse


def solution(mesh):
    rows, flat, rep = P(AXES, None), P(AXES), P()
    return jax.shard_map(
        on_device, mesh=mesh,
        in_specs=(rows, rows, flat, flat, flat, rows, flat, flat) + (rep,) * 12,
        out_specs=(rows, rows, rows), check_vma=False,
    )
```

```python
import functools
import jax
import jax.numpy as jnp
from jax import lax
from jax.experimental import pallas as pl
from jax.experimental.pallas import tpu as pltpu
from jax.sharding import PartitionSpec as P

BF, F32 = jnp.bfloat16, jnp.float32
MESH = pl.DeviceIdType.MESH
D = 512
NCD = 20
BLK = 256
WIN = 264
PIECES = ((0, 32), (32, 32), (64, 16))
ORDERS = ((3, 2, 1), (2, 1, 3), (1, 3, 2))
SEGMENTS = ((0, 1), (1, 3), (3, 5), (5, 5), (5, 5), (5, 8))


def norm_rows(x, gain, shift):
    mean = jnp.mean(x, -1, keepdims=True)
    c = x - mean
    var = jnp.mean(c * c, -1, keepdims=True)
    return c * lax.rsqrt(var + 1e-05) * gain + shift


def silu(x):
    t = 0.5 * x
    return t + t * jnp.tanh(t)


def iota(shape, dim):
    return lax.broadcasted_iota(jnp.int32, shape, dim)


def coords(a, b):
    return lax.rem(a, 2), (a // 2) * 2 + b // 16, lax.rem(b // 4, 4), lax.rem(b, 4)


def device_at(core, z, x, y):
    return ((z // 2) * 2 + core, lax.rem(z, 2) * 16 + x * 4 + y)


def edge_kernel(
    snd, rcv, csnd, crcv,
    nodes_in, lists, edges_in, cedges, crow, w1_in, b1, w2_in, b2, gain, shift,
    new_edges, msg, new_coarse, inbound,
    node_ref, w1, w2, edges, p_snd, p_rcv, g_a, g_b,
    buf0, buf1, buf2, table, rows_s, rows_r, wide, outb, bound, halo, head32,
    send_sem, recv_sem, hsend_sem, hrecv_sem, out_send, in_recv, load_sem,
):
    a, b = lax.axis_index("gx"), lax.axis_index("gy")
    me = coords(a, b)
    core = me[0]
    bufs = (buf0, buf1, buf2)
    nodes = node_ref.shape[0]

    loads = [
        pltpu.make_async_copy(src, dst, load_sem.at[k])
        for k, (src, dst) in enumerate(((nodes_in, node_ref), (w1_in, w1), (w2_in, w2), (edges_in, edges)))
    ]
    for c in loads:
        c.start()

    def peer(axis, step):
        c = list(me)
        c[axis] = lax.rem(c[axis] + step, 4)
        return device_at(*c)

    sibling = (a + 1 - 2 * core, b)
    halo_to = (
        (lax.rem(a + 1, 4), b), (lax.rem(a + 3, 4), b),
        (a, lax.rem(b + 1, 32)), (a, lax.rem(b + 31, 32)),
    )
    partners = [peer(axis, s) for axis in (1, 2, 3) for s in (1, 2, 3)] + [sibling] + list(halo_to)
    barrier = pltpu.get_barrier_semaphore()
    for p in partners:
        pl.semaphore_signal(barrier, inc=1, device_id=p, device_id_type=MESH)

    loads[0].wait()
    own = node_ref[0:32, :].astype(F32)
    for j in range(4):
        head32[pl.ds(j, 32, stride=4), :] = own[:, 128 * j:128 * (j + 1)]

    def slot(p):
        o = ORDERS[p]
        return ((core * 4 + me[o[2]]) * 4 + me[o[1]]) * 4 + me[o[0]]

    for p, (r0, n) in enumerate(PIECES):
        bufs[p][slot(p)] = head32[r0:r0 + n, :].astype(BF)

    hot = (iota((nodes, 128), 0) == lists[...]).astype(F32).astype(BF)
    bound[...] = lax.dot_general(
        hot, node_ref[...], (((0,), (0,)), ((), ())), preferred_element_type=F32).astype(BF)

    def block(p, step):
        return (core * 4 + lax.rem(me[ORDERS[p][2]] + 4 - step, 4)) * 16

    def send(p, first, size, to, k):
        part = bufs[p].at[pl.ds(first, size)]
        return pltpu.make_async_remote_copy(
            src_ref=part, dst_ref=part, send_sem=send_sem.at[p, k], recv_sem=recv_sem.at[p, k],
            device_id=to, device_id_type=MESH)

    started = []

    def go(copy):
        copy.start()
        started.append(copy)
        return copy

    def spread(p, stage):
        size = 4 ** stage
        first = slot(p) // size * size
        return [go(send(p, first, size, peer(ORDERS[p][stage], s), 3 * stage + s - 1)) for s in (2, 1, 3)]

    def across(p, first, size, k):
        return go(send(p, first, size, sibling, k))

    def arrived(copies):
        for c in copies:
            c.wait_recv()

    def project(rows, lo, tab, at, bias):
        n = rows.shape[0]
        v = jnp.dot(rows, w1[lo:lo + 512, :], preferred_element_type=F32)
        if bias is not None:
            v = v + bias
        for j in range(4):
            tab[pl.ds(at, n), j, :] = v[:, 128 * j:128 * (j + 1)]

    def project_own(lo, hi):
        @pl.loop(lo, hi)
        def _(c):
            at = pl.multiple_of(c * 256, 256)
            rows = node_ref[pl.ds(at, 256), :]
            project(rows, 512, p_snd, at, None)
            project(rows, 1024, p_rcv, at, b1[...])

    def gather(k, g, lo=0, hi=BLK):
        base = k * BLK
        for e in range(lo, hi):
            g[pl.ds(4 * e, 4), :] = p_snd[snd[base + e]] + p_rcv[rcv[base + e]]

    def first(k, g):
        x = edges[pl.ds(pl.multiple_of(k * BLK, BLK), BLK), :]
        pre = jnp.dot(x, w1[0:512, :], preferred_element_type=F32)
        pre = pre + jnp.concatenate([g[pl.ds(j, BLK, stride=4), :] for j in range(4)], 1)
        return silu(pre).astype(BF)

    def second(h):
        return jnp.dot(h, w2[...], preferred_element_type=F32) + b2[...]

    def third(k, y):
        at = pl.multiple_of(k * BLK, BLK)
        m = norm_rows(y, gain[...], shift[...])
        new_edges[pl.ds(at, BLK), :] = (edges[pl.ds(at, BLK), :].astype(F32) + m).astype(BF)
        msg[pl.ds(at, BLK), :] = m.astype(BF)

    last = edges.shape[0] // BLK - 1

    def pairs(lo, hi):
        @pl.loop(lo, hi)
        def _(i):
            half = BLK // 2
            k, n = 2 * i, jnp.minimum(2 * i + 2, last - 1)
            h_a = first(k, g_a)
            h_b = first(k + 1, g_b)
            gather(n, g_a, 0, half)
            y_a = second(h_a)
            gather(n, g_a, half, BLK)
            y_b = second(h_b)
            gather(n + 1, g_b, 0, half)
            third(k, y_a)
            gather(n + 1, g_b, half, BLK)
            third(k + 1, y_b)

    def fill(c):
        @pl.loop(0, 64)
        def _(q):
            u, v, w = q // 16, lax.rem(q // 4, 4), lax.rem(q, 4)
            for p, (r0, n) in enumerate(PIECES):
                pos = {ORDERS[p][2]: u, ORDERS[p][1]: v, ORDERS[p][0]: w}
                aa, bb = device_at(c, pos[1], pos[2], pos[3])
                table[pl.ds((aa * 32 + bb) * NCD + r0 // 4, n // 4)] = (
                    bufs[p][c * 64 + q].astype(F32).reshape(n // 4, 4, 128))

    pl.semaphore_wait(barrier, len(partners))
    one = [spread(p, 0) for p in range(3)]
    halos = []
    for k, to in enumerate(halo_to):
        halos.append(go(pltpu.make_async_remote_copy(
            src_ref=bound, dst_ref=halo.at[pl.ds(128 * k, 128)], send_sem=hsend_sem.at[k], recv_sem=hrecv_sem.at[k],
            device_id=to, device_id_type=MESH)))
    loads[1].wait()
    project_own(0, nodes // 256)
    two = []
    for p in range(3):
        arrived(one[p])
        two.append(spread(p, 1))
    for k in range(4):
        halos[k].wait_recv()
    for k in range(2):
        project(halo[256 * k:256 * (k + 1), :], 512, p_snd, nodes + 256 * k, None)
    loads[2].wait()
    loads[3].wait()
    gather(0, g_a)
    gather(1, g_b)
    pairs(*SEGMENTS[0])
    three, cross = [], []
    for p in range(3):
        arrived(two[p])
        three.append(spread(p, 2))
    for p in range(3):
        cross.append(across(p, block(p, 0), 16, 10))
    pairs(*SEGMENTS[1])
    for i, s in enumerate((2, 1, 3)):
        for p in range(3):
            three[p][i].wait_recv()
            cross.append(across(p, block(p, s), 16, 10 + s))
        if i < 2:
            pairs(*SEGMENTS[2 + i])
    fill(core)
    pairs(*SEGMENTS[4])
    arrived(cross)
    fill(1 - core)

    ce = cedges.shape[0]
    for e in range(ce):
        rows_s[pl.ds(4 * e, 4), :] = table[csnd[e]]
        rows_r[pl.ds(4 * e, 4), :] = table[crcv[e]]
    x = cedges[...]
    take = lambda ref: jnp.concatenate([ref[pl.ds(j, ce, stride=4), :] for j in range(4)], 1).astype(BF)
    pre = (
        jnp.dot(x, w1[0:512, :], preferred_element_type=F32)
        + jnp.dot(take(rows_s), w1[512:1024, :], preferred_element_type=F32)
        + jnp.dot(take(rows_r), w1[1024:1536, :], preferred_element_type=F32)
        + b1[...]
    )
    y = jnp.dot(silu(pre).astype(BF), w2[...], preferred_element_type=F32) + b2[...]
    m = norm_rows(y, gain[...], shift[...])
    new_coarse[...] = (x.astype(F32) + m).astype(BF)
    mb = m.astype(BF)

    c = crow[...]
    owner = lax.shift_right_logical(c * 52429, 20)
    local = c - owner * NCD
    own_hot = (iota((128, ce), 0) == owner).astype(F32)
    before = (iota((ce, ce), 0) < iota((ce, ce), 1)).astype(F32).astype(BF)
    counts = jnp.dot(own_hot.astype(BF), before, preferred_element_type=F32)
    rank = jnp.sum(own_hot * counts, axis=0, keepdims=True)
    for s in range(3):
        placed = jnp.where(rank == s, own_hot, 0.0).astype(BF)
        got = jnp.dot(placed, mb, preferred_element_type=F32)
        for j in range(4):
            wide[pl.ds(4 * s + j, 128, stride=16), :] = got[:, 128 * j:128 * (j + 1)]
    tags = (iota((128, ce), 0).astype(F32) == rank * 32.0 + local.astype(F32)).astype(F32).astype(BF)
    wide[pl.ds(12, 128, stride=16), :] = lax.dot_general(
        own_hot.astype(BF), tags, (((1,), (1,)), ((), ())), preferred_element_type=F32)
    for j in range(1, 4):
        wide[pl.ds(12 + j, 128, stride=16), :] = jnp.zeros((128, 128), F32)
    outb[...] = wide[...].astype(BF).reshape(128, 16, 128)

    g = a * 32 + b
    inbound[0] = outb[g]

    @pl.loop(1, 128)
    def _(k):
        to = lax.rem(g + k, 128)
        pltpu.make_async_remote_copy(
            src_ref=outb.at[to], dst_ref=inbound.at[k], send_sem=out_send, recv_sem=in_recv,
            device_id=(to // 32, lax.rem(to, 32)), device_id_type=MESH).start()

    pairs(*SEGMENTS[5])

    most = pl.ds(1, 127)
    pltpu.make_async_copy(inbound.at[most], inbound.at[most], in_recv).wait()
    pltpu.make_async_copy(outb.at[most], outb.at[most], out_send).wait()
    for k in started:
        k.wait_send()


def edge_call(snd, rcv, csnd, crcv, nodes, lists, edges, cedges, w1, b1, w2, b2, gain, shift):
    row = lambda v: v.reshape(1, -1)
    vm = pl.BlockSpec(memory_space=pltpu.VMEM)
    sm = pl.BlockSpec(memory_space=pltpu.SMEM)
    hbm = pl.BlockSpec(memory_space=pl.ANY)
    ce, E, N = cedges.shape[0], edges.shape[0], nodes.shape[0]
    return pl.pallas_call(
        edge_kernel,
        out_shape=(
            pltpu.VMEM((E, D), BF),
            pltpu.VMEM((E, D), BF),
            jax.ShapeDtypeStruct((ce, D), BF),
            jax.ShapeDtypeStruct((128, 16, 128), BF),
        ),
        in_specs=[sm] * 4 + [hbm, vm, hbm, vm, vm, hbm, vm, hbm] + [vm] * 3,
        out_specs=(vm, vm, vm, vm),
        scratch_shapes=[
            pltpu.VMEM((N, D), BF), pltpu.VMEM((3 * D, D), BF), pltpu.VMEM((D, D), BF),
            pltpu.VMEM((E, D), BF),
            pltpu.VMEM((N + 512, 4, 128), F32), pltpu.VMEM((N, 4, 128), F32),
            pltpu.VMEM((BLK * 4, 128), F32), pltpu.VMEM((BLK * 4, 128), F32),
            pltpu.VMEM((128, 32, 128), BF), pltpu.VMEM((128, 32, 128), BF), pltpu.VMEM((128, 16, 128), BF),
            pltpu.VMEM((128 * NCD, 4, 128), F32),
            pltpu.VMEM((ce * 4, 128), F32), pltpu.VMEM((ce * 4, 128), F32),
            pltpu.VMEM((2048, 128), F32), pltpu.VMEM((128, 16, 128), BF),
            pltpu.VMEM((128, D), BF), pltpu.VMEM((512, D), BF), pltpu.VMEM((128, 128), F32),
            pltpu.SemaphoreType.DMA((3, 14)), pltpu.SemaphoreType.DMA((3, 14)),
            pltpu.SemaphoreType.DMA((4,)), pltpu.SemaphoreType.DMA((4,)),
            pltpu.SemaphoreType.DMA, pltpu.SemaphoreType.DMA,
            pltpu.SemaphoreType.DMA((4,)),
        ],
        compiler_params=pltpu.CompilerParams(
            collective_id=0, has_side_effects=True, vmem_limit_bytes=54 * 2**20),
        cost_estimate=pl.CostEstimate(flops=7 * 10**9, bytes_accessed=2 * 10**7, transcendentals=2 * 10**6),
        name="edges",
    )(*(pltpu.with_memory_space_constraint(v, pltpu.HBM) for v in (
        snd, rcv, csnd, crcv, nodes, row(lists), edges, cedges, row(crcv), w1, row(b1), w2, row(b2), row(gain), row(shift))))


def node_kernel(
    rcv,
    rrow, edges, msg, coarse_in, inbound_in, nodes_in, w1_in, w2_in, b1, b2, gain, shift,
    edges_out, coarse_out, nodes_out,
    coarse, inbound, node_ref, w1, w2, new_nodes, fsum, wide,
    back_sem, small_sem, node_sem,
):
    steps, nsteps = msg.shape[0] // (2 * BLK), node_ref.shape[0] // BLK
    part = lambda i: pl.ds(2 * BLK * i, 2 * BLK)
    small = [
        pltpu.make_async_copy(src, dst, small_sem.at[k]) for k, (src, dst) in enumerate((
            (nodes_in, node_ref), (w1_in, w1), (w2_in, w2), (inbound_in, inbound), (coarse_in, coarse)))
    ]
    back = [pltpu.make_async_copy(edges.at[part(i)], edges_out.at[part(i)], back_sem.at[i]) for i in range(steps)]
    back.append(pltpu.make_async_copy(coarse, coarse_out, back_sem.at[steps]))
    for c in small + back[:steps]:
        c.start()
    fsum[...] = jnp.zeros_like(fsum)
    for i in range(steps):
        for k in (2 * i, 2 * i + 1):
            start = pl.multiple_of((rcv[k * BLK] // 8) * 8, 8)
            narrow = rcv[(k + 1) * BLK - 1] - start < 128

            def add(rows):
                ids = rrow[:, k * BLK:(k + 1) * BLK]
                hot = (ids - start == iota((rows, BLK), 0)).astype(F32).astype(BF)
                fsum[pl.ds(start, rows), :] += jnp.dot(
                    hot, msg[k * BLK:(k + 1) * BLK, :], preferred_element_type=F32)

            pl.when(narrow)(functools.partial(add, 128))
            pl.when(jnp.logical_not(narrow))(functools.partial(add, WIN))
    for c in small:
        c.wait()
    back[steps].start()
    wide[...] = inbound[...].astype(F32)
    tags = wide[pl.ds(12, 128, stride=16), :].astype(BF)
    total = fsum[0:32, :]
    for s in range(3):
        got = jnp.concatenate([wide[pl.ds(4 * s + j, 128, stride=16), :] for j in range(4)], 1).astype(BF)
        total = total + lax.dot_general(
            tags[:, 32 * s:32 * s + 32], got, (((0,), (0,)), ((), ())), preferred_element_type=F32)
    fsum[0:32, :] = total

    for c in range(nsteps):
        at = pl.ds(c * BLK, BLK)
        rows = node_ref[at, :]
        pre = (
            jnp.dot(rows, w1[0:512, :], preferred_element_type=F32)
            + jnp.dot(fsum[at, :].astype(BF), w1[512:1024, :], preferred_element_type=F32)
            + b1[...]
        )
        y = jnp.dot(silu(pre).astype(BF), w2[...], preferred_element_type=F32) + b2[...]
        new_nodes[at, :] = (rows.astype(F32) + norm_rows(y, gain[...], shift[...])).astype(BF)
        back.append(pltpu.make_async_copy(new_nodes.at[at], nodes_out.at[at], node_sem.at[c]))
        back[-1].start()
    for c in back:
        c.wait()


def node_call(rcv, edges, msg, coarse, inbound, nodes, w1, b1, w2, b2, gain, shift):
    E, N = msg.shape[0], nodes.shape[0]
    row = lambda v: v.reshape(1, -1)
    vm = pl.BlockSpec(memory_space=pltpu.VMEM)
    sm = pl.BlockSpec(memory_space=pltpu.SMEM)
    hbm = pl.BlockSpec(memory_space=pl.ANY)
    like = lambda v: pltpu.VMEM(v.shape, v.dtype)
    inbound = inbound.reshape(2048, 128)
    return pl.pallas_call(
        node_kernel,
        out_shape=tuple(jax.ShapeDtypeStruct(v.shape, BF) for v in (edges, coarse, nodes)),
        in_specs=[sm, vm, vm, vm] + [hbm] * 5 + [vm] * 4,
        out_specs=(hbm, hbm, hbm),
        scratch_shapes=[like(v) for v in (coarse, inbound, nodes, w1, w2, nodes)] + [
            pltpu.VMEM((N + WIN, D), F32), pltpu.VMEM((2048, 128), F32),
            pltpu.SemaphoreType.DMA((9,)),
            pltpu.SemaphoreType.DMA((5,)), pltpu.SemaphoreType.DMA((5,)),
        ],
        compiler_params=pltpu.CompilerParams(vmem_limit_bytes=40 * 2**20),
        cost_estimate=pl.CostEstimate(flops=3 * 10**9, bytes_accessed=16 * 10**6, transcendentals=10**6),
        name="nodes",
    )(*(pltpu.with_memory_space_constraint(v, pltpu.HBM) for v in (rcv, row(rcv))),
      *(pltpu.with_memory_space_constraint(v, pltpu.VMEM) for v in (edges, msg)),
      *(pltpu.with_memory_space_constraint(v, pltpu.HBM) for v in (
          coarse, inbound, nodes, w1, w2, row(b1), row(b2), row(gain), row(shift))))


AXES = ("gx", "gy")


def on_device(
    node_feats, edge_feats, senders, receivers, send_lists, coarse_edges, coarse_senders, coarse_receivers,
    edge_w1, edge_b1, edge_w2, edge_b2, edge_gain, edge_shift,
    node_w1, node_b1, node_w2, node_b2, node_gain, node_shift,
):
    new_edges, message, new_coarse, inbound = edge_call(
        senders, receivers, coarse_senders, coarse_receivers, node_feats, send_lists, edge_feats, coarse_edges,
        edge_w1, edge_b1, edge_w2, edge_b2, edge_gain, edge_shift)
    new_edges, new_coarse, new_nodes = node_call(
        receivers, new_edges, message, new_coarse, inbound, node_feats,
        node_w1, node_b1, node_w2, node_b2, node_gain, node_shift)
    return new_nodes, new_edges, new_coarse


def solution(mesh):
    rows, flat, rep = P(AXES, None), P(AXES), P()
    return jax.shard_map(
        on_device, mesh=mesh,
        in_specs=(rows, rows, flat, flat, flat, rows, flat, flat) + (rep,) * 12,
        out_specs=(rows, rows, rows), check_vma=False,
    )
```
